256 devices in a mesh: ep: 128 (over z, x_hi, y, core), tp: 2 (over x_lo).
Axes of the slice: x: 4 (x_hi: 2, x_lo: 2; x = x_hi * 2 + x_lo), y: 4, z: 8, core: 2. Of those that a mesh axis runs over, the one named last changes fastest.
Arguments:
- tokens: bfloat16 [256, 256, 1280], P('ep', None, 'tp'), may hold values from -400 to 400
- router: bfloat16 [1280, 128], P('tp'), may hold values from -2 to 2
- w_in: bfloat16 [128, 1280, 2560], P('ep', None, 'tp'), may hold values from -0.15625 to 0.15625
- w_out: bfloat16 [128, 2560, 1280], P('ep', 'tp'), may hold values from -0.125 to 0.125
- grad_out: bfloat16 [256, 256, 1280], P('ep', None, 'tp'), may hold values from -6 to 6
Outputs:
- grad_tokens: bfloat16 [256, 256, 1280], P('ep', None, 'tp')
- grad_router: float32 [1280, 128], P('tp')
- grad_w_in: bfloat16 [128, 1280, 2560], P('ep', None, 'tp')
The draws below stay inside these ranges and needn't reach their ends.
All inputs are finite; a program needn't handle non-finite values.
Results may differ from the reference program's by a relative error of at most 0.0095.
Values may be sent and summed in bfloat16 or wider, within the bound.
No kernel may reach another device: no remote copies, remote signals or barrier semaphores. Data moves between devices by JAX's collectives and lax.ppermute only.
A program may use at most 64 MiB of HBM per device.

```python
import math
from functools import partial
import jax
import jax.numpy as jnp
from jax import lax

D = 1280
FF = 2560
PATCHES = 256
IMAGES = 256
EXPERTS = 128


def router_columns(key, parity_weight):
    base = jax.random.fold_in(key, 11)
    values = jnp.clip(jax.random.normal(base, (D, EXPERTS), jnp.float32), -6.0, 6.0) * D ** (-0.5)
    rows = jnp.arange(D)[:, None] % 2
    cols = jnp.arange(EXPERTS)[None, :] % 2
    parity = (rows == cols).astype(jnp.float32) * math.sqrt(2.0)
    return values * (1.0 + parity_weight * parity)


def draw_router(key, part):
    columns = router_columns(key, 0.0)
    return jnp.clip(columns, -2.0, 2.0).astype(jnp.bfloat16)


def draw_tokens(key, part):
    key = jax.random.fold_in(key, 3)
    values = jnp.clip(jax.random.normal(key, (IMAGES, PATCHES, D), jnp.float32), -6.0, 6.0)
    return values.astype(jnp.bfloat16)


def level_of(key, shape, cuts, least, high):
    def one(axis_at, blocks):
        draws = jax.random.uniform(jax.random.fold_in(jax.random.fold_in(key, 6), axis_at), (blocks,), jnp.float32, least / len(cuts), high / len(cuts))
        return jnp.repeat(jnp.exp(draws), shape[axis_at] // blocks).reshape((-1,) + (1,) * (len(shape) - axis_at - 1))

    level = one(*cuts[0])
    for cut in cuts[1:]:
        level = level * one(*cut)
    return level


def noise(key, shape, deviation, reach, cuts=(), dtype=jnp.bfloat16):
    drawn = deviation * jax.random.normal(key, shape, jnp.float32)
    if cuts:
        drawn = drawn * level_of(key, shape, cuts, -0.22, 0.18)
    return jnp.clip(drawn, -reach, reach).astype(dtype)


def setup_inputs(seed: int = 0) -> dict:
    key_of = jax.random.split(jax.random.key(seed), 6)
    return {
        "tokens": draw_tokens(jax.random.fold_in(key_of[5], 71), 0),
        "router": draw_router(jax.random.fold_in(key_of[5], 71), 0),
        "w_in": noise(key_of[2], (EXPERTS, D, FF), D ** -0.5, 0.15625, ((0, 128), (2, 2))),
        "w_out": noise(key_of[3], (EXPERTS, FF, D), FF ** -0.5, 0.125, ((0, 128), (1, 2))),
        "grad_out": noise(key_of[4], (IMAGES, PATCHES, D), 1.0, 6.0, ((0, 128), (2, 2))),
    }


def expert_backward(items):
    slot_in, slot_grad, weight_in, weight_out = items
    pre = jnp.dot(slot_in, weight_in, preferred_element_type=jnp.float32)
    act, back = jax.vjp(partial(jax.nn.gelu, approximate=True), pre)
    slot_out = jnp.dot(act.astype(jnp.bfloat16), weight_out, preferred_element_type=jnp.float32).astype(jnp.bfloat16)
    act_grad = jnp.dot(slot_grad, weight_out.T, preferred_element_type=jnp.float32)
    pre_grad = back(act_grad)[0].astype(jnp.bfloat16)
    grad_weight = jnp.dot(slot_in.T, pre_grad, preferred_element_type=jnp.float32).astype(jnp.bfloat16)
    slot_in_grad = jnp.dot(pre_grad, weight_in.T, preferred_element_type=jnp.float32).astype(jnp.bfloat16)
    return (slot_out, grad_weight, slot_in_grad)

def reference(tokens, router, w_in, w_out, grad_out):
    tok32 = tokens.astype(jnp.float32)
    logits = jnp.einsum('bmd,de->bme', tok32, router.astype(jnp.float32))
    dispatch = jax.nn.softmax(logits, axis=1)
    combine = jax.nn.softmax(logits, axis=2)
    dispatch_b = dispatch.astype(jnp.bfloat16).astype(jnp.float32)
    combine_b = combine.astype(jnp.bfloat16).astype(jnp.float32)
    slot_in = jnp.einsum('bme,bmd->ebd', dispatch_b, tok32).astype(jnp.bfloat16)
    slot_grad = jnp.einsum('bme,bmd->ebd', combine_b, grad_out.astype(jnp.float32)).astype(jnp.bfloat16)
    slot_out, grad_w_in, slot_in_grad = lax.map(expert_backward, (slot_in, slot_grad, w_in, w_out))
    combine_dot = jnp.einsum('bmd,ebd->bme', grad_out.astype(jnp.float32), slot_out.astype(jnp.float32))
    grad_in32 = slot_in_grad.astype(jnp.float32)
    dispatch_dot = jnp.einsum('bmd,ebd->bme', tok32, grad_in32)
    logit_grad = combine * (combine_dot - lax.optimization_barrier(jnp.sum(combine * combine_dot, axis=2, keepdims=True)))
    logit_grad = logit_grad + dispatch * (dispatch_dot - lax.optimization_barrier(jnp.sum(dispatch * dispatch_dot, axis=1, keepdims=True)))
    logit_b = logit_grad.astype(jnp.bfloat16).astype(jnp.float32)
    grad_tokens = jnp.einsum('bme,ebd->bmd', dispatch_b, grad_in32)
    grad_tokens = grad_tokens + jnp.einsum('bme,de->bmd', logit_b, router.astype(jnp.float32))
    grad_router = jnp.einsum('bmd,bme->de', tok32, logit_b)
    return (grad_tokens.astype(jnp.bfloat16), grad_router, grad_w_in)
```

```python
from functools import partial

import jax
import jax.numpy as jnp
from jax import lax
from jax.sharding import Mesh, PartitionSpec as P

AXES = ("z", "x_hi", "y", "core", "tp")
CHIPS = ("z", "x_hi", "y")
F32 = jnp.float32
BF16 = jnp.bfloat16


def swap(x, axis):
    return lax.ppermute(x, axis, [(0, 1), (1, 0)])


def pick(flag, a, b):
    return jnp.where(flag, a, b)


def to_experts(slots):
    core = lax.axis_index("core")
    by_core = slots.reshape(64, 2, 2, slots.shape[-1])
    keep = pick(core == 0, by_core[:, 0], by_core[:, 1])
    send = pick(core == 0, by_core[:, 1], by_core[:, 0])
    both = jnp.concatenate([keep, swap(send, "core")], axis=1)
    got = lax.all_to_all(both, CHIPS, split_axis=0, concat_axis=0, tiled=True)
    return got.reshape(256, slots.shape[-1])


def to_images(rows):
    core = lax.axis_index("core")
    got = lax.all_to_all(
        rows.reshape(64, 4, rows.shape[-1]), CHIPS, split_axis=0, concat_axis=0, tiled=True
    )
    keep = got[:, :2]
    other = swap(got[:, 2:], "core")
    by_core = jnp.stack([pick(core == 0, keep, other), pick(core == 0, other, keep)], axis=1)
    return by_core.reshape(128, 2, rows.shape[-1])


def widen(half):
    tp = lax.axis_index("tp")
    other = swap(half, "tp")
    return pick(
        tp == 0,
        jnp.concatenate([half, other], axis=1),
        jnp.concatenate([other, half], axis=1),
    )


def sum_halves(part):
    tp = lax.axis_index("tp")
    n = part.shape[1] // 2
    keep = pick(tp == 0, part[:, :n], part[:, n:])
    send = pick(tp == 0, part[:, n:], part[:, :n]).astype(BF16)
    return (keep + swap(send, "tp").astype(F32)).astype(BF16)


def sum_over_ep(part):
    core = lax.axis_index("core")
    n = part.shape[0] // 2
    keep = pick(core == 0, part[:n], part[n:])
    send = pick(core == 0, part[n:], part[:n])
    half = (keep + swap(send, "core")).reshape(8, n // 8, -1)
    got = lax.all_to_all(half, ("x_hi", "y"), split_axis=0, concat_axis=0, tiled=True)
    chunk = jnp.sum(got, axis=0)
    same = jnp.broadcast_to(chunk[None], (8,) + chunk.shape)
    got = lax.all_to_all(same, "z", split_axis=0, concat_axis=0, tiled=True)
    chunk = jnp.sum(got, axis=0)
    same = jnp.broadcast_to(chunk[None], (8,) + chunk.shape)
    got = lax.all_to_all(same, ("x_hi", "y"), split_axis=0, concat_axis=0, tiled=True)
    half = got.reshape(n, -1)
    other = swap(half, "core")
    return pick(
        core == 0,
        jnp.concatenate([half, other], axis=0),
        jnp.concatenate([other, half], axis=0),
    )


def on_device(tokens, router, w_in, w_out, grad_out):
    part = jnp.einsum("bmd,de->bme", tokens, router, preferred_element_type=F32)
    logits = part + swap(part, "tp")
    dispatch = jax.nn.softmax(logits, axis=1)
    combine = jax.nn.softmax(logits, axis=2)
    dispatch_b = dispatch.astype(BF16)
    combine_b = combine.astype(BF16)
    slot_half = jnp.einsum(
        "bme,bmd->ebd", dispatch_b, tokens, preferred_element_type=F32
    ).astype(BF16)
    grad_half = jnp.einsum(
        "bme,bmd->ebd", combine_b, grad_out, preferred_element_type=F32
    ).astype(BF16)
    slot_in = widen(to_experts(slot_half))
    slot_grad = widen(to_experts(grad_half))
    weight_in = w_in[0]
    weight_out = w_out[0]
    pre = jnp.dot(slot_in, weight_in, preferred_element_type=F32)
    act, back = jax.vjp(partial(jax.nn.gelu, approximate=True), pre)
    out_part = jnp.dot(act.astype(BF16), weight_out, preferred_element_type=F32)
    slot_out = to_images(sum_halves(out_part))
    act_grad = jnp.einsum("bd,fd->bf", slot_grad, weight_out, preferred_element_type=F32)
    pre_grad = back(act_grad)[0].astype(BF16)
    in_part = jnp.einsum("bf,df->bd", pre_grad, weight_in, preferred_element_type=F32)
    slot_in_grad = to_images(sum_halves(in_part))
    grad_weight = jnp.einsum(
        "bd,bf->df", slot_in, pre_grad, preferred_element_type=F32
    ).astype(BF16)
    combine_part = jnp.einsum("bmd,ebd->bme", grad_out, slot_out, preferred_element_type=F32)
    combine_dot = combine_part + swap(combine_part, "tp")
    dispatch_part = jnp.einsum("bmd,ebd->bme", tokens, slot_in_grad, preferred_element_type=F32)
    dispatch_dot = dispatch_part + swap(dispatch_part, "tp")
    logit_grad = combine * (combine_dot - jnp.sum(combine * combine_dot, axis=2, keepdims=True))
    logit_grad = logit_grad + dispatch * (
        dispatch_dot - jnp.sum(dispatch * dispatch_dot, axis=1, keepdims=True)
    )
    logit_b = logit_grad.astype(BF16)
    router_part = jnp.einsum("bmd,bme->de", tokens, logit_b, preferred_element_type=F32)
    grad_router = sum_over_ep(router_part)
    grad_tokens = jnp.einsum(
        "bme,ebd->bmd", dispatch_b, slot_in_grad, preferred_element_type=F32
    )
    grad_tokens = grad_tokens + jnp.einsum(
        "bme,de->bmd", logit_b, router, preferred_element_type=F32
    )
    return grad_tokens.astype(BF16), grad_router, grad_weight[None]


def solution(mesh):
    fine = Mesh(mesh.devices.reshape(8, 2, 4, 2, 2), AXES)
    ep = ("z", "x_hi", "y", "core")
    return jax.shard_map(
        on_device,
        mesh=fine,
        in_specs=(
            P(ep, None, "tp"),
            P("tp", None),
            P(ep, None, "tp"),
            P(ep, "tp", None),
            P(ep, None, "tp"),
        ),
        out_specs=(P(ep, None, "tp"), P("tp", None), P(ep, None, "tp")),
        check_vma=False,
    )
```

```python
import jax
import jax.numpy as jnp
from jax import lax
from jax.experimental import pallas as pl
from jax.experimental.pallas import tpu as pltpu
from jax.sharding import Mesh, PartitionSpec as P

AXES = ("z", "x_hi", "y", "core", "tp")
CHIPS = ("z", "x_hi", "y")
F32 = jnp.float32
BF16 = jnp.bfloat16
I32 = jnp.int32
NQ = 64
B = 2
M = 256
E = 128
H = 640
D = 1280
FH = 1280
CH = 256
MIB = 1 << 20

SMEM = pl.BlockSpec(memory_space=pltpu.SMEM)
VMEM = pl.BlockSpec(memory_space=pltpu.VMEM)


def dot(a, b):
    return jnp.dot(a, b, preferred_element_type=F32)


def dot_t(a, b):
    return lax.dot_general(a, b, (((1,), (1,)), ((), ())), preferred_element_type=F32)


def t_dot(a, b):
    return lax.dot_general(a, b, (((0,), (0,)), ((), ())), preferred_element_type=F32)


def rows_cols(rows, cols):
    return (
        lax.broadcasted_iota(I32, (rows, cols), 0),
        lax.broadcasted_iota(I32, (rows, cols), 1),
    )


def ones_where(mask):
    return jnp.where(mask, 1.0, 0.0).astype(BF16)


def expert_order(core):
    e, p = rows_cols(E, E)
    return ones_where(e == 2 * (p & 63) + (core ^ (p >> 6)))


def call(kernel, outs, flops, nbytes, limit=None):
    def run(*args):
        return pl.pallas_call(
            kernel,
            out_shape=[jax.ShapeDtypeStruct(s, d) for s, d in outs],
            in_specs=[SMEM if a.dtype == I32 else VMEM for a in args],
            out_specs=[VMEM for _ in outs],
            cost_estimate=pl.CostEstimate(
                flops=int(flops), bytes_accessed=int(nbytes), transcendentals=0
            ),
            compiler_params=pltpu.CompilerParams(vmem_limit_bytes=(limit or 24) * MIB),
        )(*args)

    return run


def logits_kernel(ids, tokens, router, part, ordered):
    r = dot(router[...], expert_order(ids[0])).astype(BF16)
    ordered[...] = r
    for b in range(B):
        part[b * M : (b + 1) * M, :] = dot(tokens[b], r)


def slots_kernel(part, other, tokens, grad, dispatch, combine, keep, send):
    for b in range(B):
        rows = slice(b * M, (b + 1) * M)
        logits = part[rows, :] + other[rows, :]
        up = jnp.exp(logits - jnp.max(logits, axis=0, keepdims=True))
        d = up / jnp.sum(up, axis=0, keepdims=True)
        up = jnp.exp(logits - jnp.max(logits, axis=1, keepdims=True))
        c = up / jnp.sum(up, axis=1, keepdims=True)
        dispatch[rows, :] = d
        combine[rows, :] = c
        for a, (w, x) in enumerate(((d, tokens), (c, grad))):
            s = t_dot(w.astype(BF16), x[b]).astype(BF16)
            k = 2 * a + b
            keep[k * NQ : (k + 1) * NQ, :] = s[:NQ]
            send[k * NQ : (k + 1) * NQ, :] = s[NQ:]


def pack_kernel(keep, got, out):
    i, j = rows_cols(8 * NQ, 4 * NQ)
    for s, x in enumerate((keep, got)):
        to = ones_where((j == (i & 3) * NQ + (i >> 3)) & (((i >> 2) & 1) == s))
        part = dot(to, x[...])
        total = part if s == 0 else total + part
    out[...] = total.astype(BF16)


def split_kernel(rows, slot_in, slot_grad):
    n, i = rows_cols(4 * NQ, 8 * NQ)
    for a, out in enumerate((slot_in, slot_grad)):
        src = (n & 63) * 8 + ((n >> 7) & 1) * 4 + a * 2 + ((n >> 6) & 1)
        out[...] = dot(ones_where(i == src), rows[...]).astype(BF16)


def both_halves(ids):
    t = ids[1]
    return (
        pl.ds(pl.multiple_of(t * H, 128), H),
        pl.ds(pl.multiple_of((1 - t) * H, 128), H),
    )


def up_kernel(ids, own, other, w_in, w_out, slope, out_keep, out_send):
    mine, theirs = both_halves(ids)
    x, y = own[...], other[...]
    keep = jnp.zeros((4 * NQ, H), F32)
    sent = jnp.zeros((4 * NQ, H), F32)
    for f in range(0, FH, CH):
        cols = slice(f, f + CH)
        v = dot(x, w_in[0, mine, cols]) + dot(y, w_in[0, theirs, cols])
        sq = v * v
        t = jnp.tanh(0.7978845608 * (v + 0.044715 * v * sq))
        act = (0.5 * v * (1.0 + t)).astype(BF16)
        slope[:, cols] = 0.5 * (1.0 + t) + 0.5 * v * (1.0 - t * t) * (
            0.7978845608 * (1.0 + 0.134145 * sq)
        )
        keep = keep + dot(act, w_out[0, cols, mine])
        sent = sent + dot(act, w_out[0, cols, theirs])
    out_keep[...] = keep
    out_send[...] = sent.astype(BF16)


def down_kernel(ids, own, other, slope, w_in, w_out, pre_grad, in_keep, in_send):
    mine, theirs = both_halves(ids)
    x, y = own[...], other[...]
    keep = jnp.zeros((4 * NQ, H), F32)
    sent = jnp.zeros((4 * NQ, H), F32)
    for f in range(0, FH, CH):
        cols = slice(f, f + CH)
        g = dot_t(x, w_out[0, cols, mine]) + dot_t(y, w_out[0, cols, theirs])
        g = (g * slope[:, cols]).astype(BF16)
        pre_grad[:, cols] = g
        keep = keep + dot_t(g, w_in[0, mine, cols])
        sent = sent + dot_t(g, w_in[0, theirs, cols])
    in_keep[...] = keep
    in_send[...] = sent.astype(BF16)


def weight_kernel(ids, own, other, pre_grad, out):
    for x, rows in zip((own, other), both_halves(ids)):
        out[0, rows, :] = t_dot(x[...], pre_grad[...]).astype(BF16)


def merge_kernel(out_keep, out_got, in_keep, in_got, out):
    i, n = rows_cols(8 * NQ, 4 * NQ)
    for a, (x, y) in enumerate(((out_keep, out_got), (in_keep, in_got))):
        r = (x[...] + y[...].astype(F32)).astype(BF16)
        src = ((i >> 2) & 1) * 128 + (i & 1) * 64 + (i >> 3)
        part = dot(ones_where((n == src) & (((i >> 1) & 1) == a)), r)
        total = part if a == 0 else total + part
    out[...] = total.astype(BF16)


def unpack_kernel(rows, own, send):
    n, i = rows_cols(4 * NQ, 8 * NQ)
    for s, out in enumerate((own, send)):
        src = (n & 63) * 8 + s * 4 + (n >> 6)
        out[...] = dot(ones_where(i == src), rows[...]).astype(BF16)


def slots_of(own, got, a, b):
    rows = slice((2 * a + b) * NQ, (2 * a + b + 1) * NQ)
    return jnp.concatenate([own[rows, :], got[rows, :]], axis=0)


def dots_kernel(own, got, tokens, grad, part, send):
    for a, x in enumerate((grad, tokens)):
        for b in range(B):
            p = dot_t(x[b], slots_of(own, got, a, b))
            rows = slice((2 * a + b) * M, (2 * a + b + 1) * M)
            part[rows, :] = p
            send[rows, :] = p.astype(BF16)


def first_kernel(own, got, dispatch, out):
    for b in range(B):
        w = dispatch[b * M : (b + 1) * M, :].astype(BF16)
        out[b] = dot(w, slots_of(own, got, 1, b))


def logit_kernel(ids, part, got, dispatch, combine, tokens, logit, keep, send, whole):
    back = expert_order(ids[0])
    total = jnp.zeros((E, H), F32)
    for b in range(B):
        rows = slice(b * M, (b + 1) * M)
        c, d = combine[rows, :], dispatch[rows, :]
        x = part[rows, :] + got[rows, :].astype(F32)
        low = slice((B + b) * M, (B + b + 1) * M)
        y = part[low, :] + got[low, :].astype(F32)
        g = c * (x - jnp.sum(c * x, axis=1, keepdims=True))
        g = (g + d * (y - jnp.sum(d * y, axis=0, keepdims=True))).astype(BF16)
        logit[rows, :] = g
        plain = dot_t(g, back).astype(BF16)
        total = total + t_dot(plain, tokens[b])
    whole[...] = jnp.transpose(total)
    c = ids[0]
    n = H // 2
    keep[...] = whole[pl.ds(pl.multiple_of(c * n, 8), n), :]
    send[...] = whole[pl.ds(pl.multiple_of((1 - c) * n, 8), n), :]


def tokens_kernel(first, logit, router, out):
    for b in range(B):
        g = first[b] + dot_t(logit[b * M : (b + 1) * M, :], router[...])
        out[b] = g.astype(BF16)


def add_kernel(x, y, out):
    out[...] = x[...] + y[...]


def spread_kernel(x, out):
    total = x[0]
    for i in range(1, 8):
        total = total + x[i]
    for i in range(8):
        out[i] = total


def join_kernel(ids, half, other, out):
    c = ids[0]
    n = H // 2
    out[pl.ds(pl.multiple_of(c * n, 8), n), :] = half[...]
    out[pl.ds(pl.multiple_of((1 - c) * n, 8), n), :] = other[...]


def swap(x, axis):
    return lax.ppermute(x, axis, [(0, 1), (1, 0)])


def exchange(x, axes):
    return lax.all_to_all(x, axes, split_axis=0, concat_axis=0, tiled=True)


def on_device(tokens, router, w_in, w_out, grad_out):
    ids = jnp.stack([lax.axis_index("core"), lax.axis_index("tp")]).astype(I32)
    part, ordered = call(
        logits_kernel, [((B * M, E), F32), ((H, E), BF16)], 2 * 512 * H * E, 1e6
    )(ids, tokens, router)
    other = swap(part, "tp")
    half = ((4 * NQ, H), BF16)
    half32 = ((4 * NQ, H), F32)
    dispatch, combine, keep, send = call(
        slots_kernel, [((B * M, E), F32)] * 2 + [half] * 2, 4 * 512 * H * E, 3e6
    )(part, other, tokens, grad_out)
    got = swap(send, "core")
    (packed,) = call(pack_kernel, [((8 * NQ, H), BF16)], 3e8, 1.3e6)(keep, got)
    rows = exchange(packed.reshape(NQ, 8, H), CHIPS).reshape(8 * NQ, H)
    in_own, grad_own = call(split_kernel, [half] * 2, 3e8, 1.3e6)(rows)
    in_other = swap(in_own, "tp")
    grad_other = swap(grad_own, "tp")
    slope, out_keep, out_send = call(
        up_kernel, [((4 * NQ, FH), F32), half32, half], 1.7e9, 1e7
    )(ids, in_own, in_other, w_in, w_out)
    out_got = swap(out_send, "tp")
    pre_grad, in_keep, in_send = call(
        down_kernel, [((4 * NQ, FH), BF16), half32, half], 1.7e9, 1e7
    )(ids, grad_own, grad_other, slope, w_in, w_out)
    in_got = swap(in_send, "tp")
    (merged,) = call(merge_kernel, [((8 * NQ, H), BF16)], 3e8, 2.6e6)(
        out_keep, out_got, in_keep, in_got
    )
    rows = exchange(merged.reshape(NQ, 8, H), CHIPS).reshape(8 * NQ, H)
    (grad_weight,) = call(weight_kernel, [((1, D, FH), BF16)], 8.4e8, 5e6)(
        ids, in_own, in_other, pre_grad
    )
    own, send = call(unpack_kernel, [half] * 2, 3e8, 1.3e6)(rows)
    got = swap(send, "core")
    part, send = call(
        dots_kernel, [((2 * B * M, E), F32), ((2 * B * M, E), BF16)], 4 * 512 * H * E, 3e6
    )(own, got, tokens, grad_out)
    dots_got = swap(send, "tp")
    (first,) = call(first_kernel, [((B, M, H), F32)], 2 * 512 * H * E, 2e6)(own, got, dispatch)
    third = ((H // 2, E), F32)
    logit, keep, send = pl.pallas_call(
        logit_kernel,
        out_shape=[
            jax.ShapeDtypeStruct((B * M, E), BF16),
            jax.ShapeDtypeStruct(*third),
            jax.ShapeDtypeStruct(*third),
        ],
        in_specs=[SMEM] + [VMEM] * 5,
        out_specs=[VMEM] * 3,
        scratch_shapes=[pltpu.VMEM((H, E), F32)],
        cost_estimate=pl.CostEstimate(
            flops=2 * 512 * H * E, bytes_accessed=3000000, transcendentals=0
        ),
        compiler_params=pltpu.CompilerParams(vmem_limit_bytes=24 * MIB),
    )(ids, part, dots_got, dispatch, combine, tokens)
    got = swap(send, "core")
    (summed,) = call(add_kernel, [third], 1e5, 5e5)(keep, got)
    eight = ((8, H // 16, E), F32)
    summed = exchange(summed.reshape(eight[0]), ("x_hi", "y"))
    (summed,) = call(spread_kernel, [eight], 1e5, 5e5)(summed)
    summed = exchange(summed, "z")
    (summed,) = call(spread_kernel, [eight], 1e5, 5e5)(summed)
    summed = exchange(summed, ("x_hi", "y")).reshape(H // 2, E)
    (grad_tokens,) = call(tokens_kernel, [((B, M, H), BF16)], 2 * 512 * H * E, 3e6)(
        first, logit, ordered
    )
    (grad_router,) = call(join_kernel, [((H, E), F32)], 1e5, 7e5)(
        ids, summed, swap(summed, "core")
    )
    return grad_tokens, grad_router, grad_weight


def solution(mesh):
    fine = Mesh(mesh.devices.reshape(8, 2, 4, 2, 2), AXES)
    ep = ("z", "x_hi", "y", "core")
    return jax.shard_map(
        on_device,
        mesh=fine,
        in_specs=(
            P(ep, None, "tp"),
            P("tp", None),
            P(ep, None, "tp"),
            P(ep, "tp", None),
            P(ep, None, "tp"),
        ),
        out_specs=(P(ep, None, "tp"), P("tp", None), P(ep, None, "tp")),
        check_vma=False,
    )
```

```python
import jax
import jax.numpy as jnp
from jax import lax
from jax.experimental import pallas as pl
from jax.experimental.pallas import tpu as pltpu
from jax.sharding import Mesh, PartitionSpec as P

AXES = ("z", "x_hi", "y", "core", "tp")
CHIPS = ("z", "x_hi", "y")
F32 = jnp.float32
BF16 = jnp.bfloat16
I32 = jnp.int32
NQ = 64
B = 2
M = 256
E = 128
H = 640
D = 1280
FH = 1280
CH = 256
MIB = 1 << 20

SMEM = pl.BlockSpec(memory_space=pltpu.SMEM)
VMEM = pl.BlockSpec(memory_space=pltpu.VMEM)
HBM = pl.BlockSpec(memory_space=pltpu.HBM)


def dot(a, b):
    return jnp.dot(a, b, preferred_element_type=F32)


def dot_t(a, b):
    return lax.dot_general(a, b, (((1,), (1,)), ((), ())), preferred_element_type=F32)


def t_dot(a, b):
    return lax.dot_general(a, b, (((0,), (0,)), ((), ())), preferred_element_type=F32)


def rows_cols(rows, cols):
    return (
        lax.broadcasted_iota(I32, (rows, cols), 0),
        lax.broadcasted_iota(I32, (rows, cols), 1),
    )


def ones_where(mask):
    return jnp.where(mask, 1.0, 0.0).astype(BF16)


def expert_order(core):
    e, p = rows_cols(E, E)
    return ones_where(e == 2 * (p & 63) + (core ^ (p >> 6)))


def call(kernel, outs, flops, nbytes, hbm=(), scratch=(), limit=24):
    def run(*args):
        args = [
            pltpu.with_memory_space_constraint(a, pltpu.HBM) if i in hbm else a
            for i, a in enumerate(args)
        ]
        return pl.pallas_call(
            kernel,
            out_shape=[jax.ShapeDtypeStruct(s, d) for s, d in outs],
            in_specs=[
                SMEM if a.dtype == I32 else HBM if i in hbm else VMEM for i, a in enumerate(args)
            ],
            out_specs=[VMEM for _ in outs],
            scratch_shapes=list(scratch),
            cost_estimate=pl.CostEstimate(
                flops=int(flops), bytes_accessed=int(nbytes), transcendentals=0
            ),
            compiler_params=pltpu.CompilerParams(vmem_limit_bytes=limit * MIB),
        )(*args)

    return run


def logits_kernel(ids, tokens_hbm, router_hbm, part, ordered, tokens, router, sems):
    copies = [
        pltpu.make_async_copy(tokens_hbm, tokens, sems.at[0]),
        pltpu.make_async_copy(router_hbm, router, sems.at[1]),
    ]
    for c in copies:
        c.start()
    order = expert_order(ids[0])
    copies[1].wait()
    r = dot(router[...], order).astype(BF16)
    ordered[...] = r
    copies[0].wait()
    for b in range(B):
        part[b * M : (b + 1) * M, :] = dot(tokens[b], r)


def fetch_kernel(*refs):
    n = len(refs) // 2
    sems = refs[-1]
    copies = [pltpu.make_async_copy(refs[i], refs[n + i], sems.at[i]) for i in range(n)]
    for c in copies:
        c.start()
    for c in copies:
        c.wait()


def slots_kernel(part, other, tokens, grad, dispatch, combine, keep, send):
    for b in range(B):
        rows = slice(b * M, (b + 1) * M)
        logits = part[rows, :] + other[rows, :]
        up = jnp.exp(logits - jnp.max(logits, axis=0, keepdims=True))
        d = up / jnp.sum(up, axis=0, keepdims=True)
        up = jnp.exp(logits - jnp.max(logits, axis=1, keepdims=True))
        c = up / jnp.sum(up, axis=1, keepdims=True)
        dispatch[rows, :] = d
        combine[rows, :] = c
        for a, (w, x) in enumerate(((d, tokens), (c, grad))):
            s = t_dot(w.astype(BF16), x[b]).astype(BF16)
            k = 2 * a + b
            keep[k * NQ : (k + 1) * NQ, :] = s[:NQ]
            send[k * NQ : (k + 1) * NQ, :] = s[NQ:]


def pack_kernel(keep, got, out):
    i, j = rows_cols(8 * NQ, 4 * NQ)
    for s, x in enumerate((keep, got)):
        to = ones_where((j == (i & 3) * NQ + (i >> 3)) & (((i >> 2) & 1) == s))
        part = dot(to, x[...])
        total = part if s == 0 else total + part
    out[...] = total.astype(BF16)


def split_kernel(rows, slot_in, slot_grad):
    n, i = rows_cols(4 * NQ, 8 * NQ)
    for a, out in enumerate((slot_in, slot_grad)):
        src = (n & 63) * 8 + ((n >> 7) & 1) * 4 + a * 2 + ((n >> 6) & 1)
        out[...] = dot(ones_where(i == src), rows[...]).astype(BF16)


def both_halves(ids):
    t = ids[1]
    return (
        pl.ds(pl.multiple_of(t * H, 128), H),
        pl.ds(pl.multiple_of((1 - t) * H, 128), H),
    )


def up_kernel(ids, own, other, w_in, w_out, slope, out_keep, out_send):
    mine, theirs = both_halves(ids)
    x, y = own[...], other[...]
    keep = jnp.zeros((4 * NQ, H), F32)
    sent = jnp.zeros((4 * NQ, H), F32)
    for f in range(0, FH, CH):
        cols = slice(f, f + CH)
        v = dot(x, w_in[0, mine, cols]) + dot(y, w_in[0, theirs, cols])
        sq = v * v
        t = jnp.tanh(0.7978845608 * (v + 0.044715 * v * sq))
        act = (0.5 * v * (1.0 + t)).astype(BF16)
        slope[:, cols] = 0.5 * (1.0 + t) + 0.5 * v * (1.0 - t * t) * (
            0.7978845608 * (1.0 + 0.134145 * sq)
        )
        keep = keep + dot(act, w_out[0, cols, mine])
        sent = sent + dot(act, w_out[0, cols, theirs])
    out_keep[...] = keep
    out_send[...] = sent.astype(BF16)


def down_kernel(ids, own, other, slope, w_in, w_out, pre_grad, in_keep, in_send):
    mine, theirs = both_halves(ids)
    x, y = own[...], other[...]
    keep = jnp.zeros((4 * NQ, H), F32)
    sent = jnp.zeros((4 * NQ, H), F32)
    for f in range(0, FH, CH):
        cols = slice(f, f + CH)
        g = dot_t(x, w_out[0, cols, mine]) + dot_t(y, w_out[0, cols, theirs])
        g = (g * slope[:, cols]).astype(BF16)
        pre_grad[:, cols] = g
        keep = keep + dot_t(g, w_in[0, mine, cols])
        sent = sent + dot_t(g, w_in[0, theirs, cols])
    in_keep[...] = keep
    in_send[...] = sent.astype(BF16)


def weight_kernel(ids, own, other, pre_grad, out, done):
    for x, rows in zip((own, other), both_halves(ids)):
        out[0, rows, :] = t_dot(x[...], pre_grad[...]).astype(BF16)
    done[...] = jnp.zeros(done.shape, F32)


def merge_kernel(out_keep, out_got, in_keep, in_got, done, out):
    i, n = rows_cols(8 * NQ, 4 * NQ)
    for a, (x, y) in enumerate(((out_keep, out_got), (in_keep, in_got))):
        r = (x[...] + y[...].astype(F32)).astype(BF16)
        src = ((i >> 2) & 1) * 128 + (i & 1) * 64 + (i >> 3)
        part = dot(ones_where((n == src) & (((i >> 1) & 1) == a)), r)
        total = part if a == 0 else total + part
    out[...] = total.astype(BF16)


def unpack_kernel(rows, own, send):
    n, i = rows_cols(4 * NQ, 8 * NQ)
    for s, out in enumerate((own, send)):
        src = (n & 63) * 8 + s * 4 + (n >> 6)
        out[...] = dot(ones_where(i == src), rows[...]).astype(BF16)


def slots_of(own, got, a, b):
    rows = slice((2 * a + b) * NQ, (2 * a + b + 1) * NQ)
    return jnp.concatenate([own[rows, :], got[rows, :]], axis=0)


def dots_kernel(own, got, tokens, grad, dispatch, combine, part, send):
    for b in range(B):
        rows = slice(b * M, (b + 1) * M)
        c, d = combine[rows, :], dispatch[rows, :]
        x = dot_t(grad[b], slots_of(own, got, 0, b))
        y = dot_t(tokens[b], slots_of(own, got, 1, b))
        g = c * (x - jnp.sum(c * x, axis=1, keepdims=True))
        g = g + d * (y - jnp.sum(d * y, axis=0, keepdims=True))
        part[rows, :] = g
        send[rows, :] = g.astype(BF16)


def first_kernel(own, got, dispatch, out, done):
    for b in range(B):
        w = dispatch[b * M : (b + 1) * M, :].astype(BF16)
        out[b] = dot(w, slots_of(own, got, 1, b))
    done[...] = jnp.zeros(done.shape, F32)


def logit_kernel(ids, part, got, tokens, done, logit, keep, send, whole):
    g = (part[...] + got[...].astype(F32)).astype(BF16)
    logit[...] = g
    plain = dot_t(g, expert_order(ids[0])).astype(BF16)
    total = t_dot(plain[:M], tokens[0]) + t_dot(plain[M:], tokens[1])
    whole[...] = jnp.transpose(total)
    c = ids[0]
    n = H // 16
    for i in range(8):
        keep[i] = whole[pl.ds(pl.multiple_of((2 * i + c) * n, 8), n), :]
        send[i] = whole[pl.ds(pl.multiple_of((2 * i + 1 - c) * n, 8), n), :]


def tokens_kernel(first, logit, router, out, done):
    for b in range(B):
        g = first[b] + dot_t(logit[b * M : (b + 1) * M, :], router[...])
        out[b] = g.astype(BF16)
    done[...] = jnp.zeros(done.shape, F32)


def add_kernel(x, y, done, out):
    out[...] = x[...] + y[...]


def spread_kernel(x, out):
    total = x[0]
    for i in range(1, 8):
        total = total + x[i]
    for i in range(out.shape[0]):
        out[i] = total


def swap(x, axis):
    return lax.ppermute(x, axis, [(0, 1), (1, 0)])


def exchange(x, axes):
    return lax.all_to_all(x, axes, split_axis=0, concat_axis=0, tiled=True)


def on_device(tokens, router, w_in, w_out, grad_out):
    ids = jnp.stack([lax.axis_index("core"), lax.axis_index("tp")]).astype(I32)
    half = ((4 * NQ, H), BF16)
    half32 = ((4 * NQ, H), F32)
    done = ((8, E), F32)
    small = 2 * B * M * H * E
    part, ordered, tokens = call(
        logits_kernel,
        [((B * M, E), F32), ((H, E), BF16), ((B, M, H), BF16)],
        small,
        1e6,
        hbm=(1, 2),
        scratch=[pltpu.VMEM((H, E), BF16), pltpu.SemaphoreType.DMA((2,))],
    )(ids, tokens, router)
    other = swap(part, "tp")
    grad_out, w_in, w_out = call(
        fetch_kernel,
        [((B, M, H), BF16), ((1, D, FH), BF16), ((1, FH, D), BF16)],
        0,
        1.4e7,
        hbm=(0, 1, 2),
        scratch=[pltpu.SemaphoreType.DMA((3,))],
    )(grad_out, w_in, w_out)
    dispatch, combine, keep, send = call(
        slots_kernel, [((B * M, E), F32)] * 2 + [half] * 2, 2 * small, 3e6
    )(part, other, tokens, grad_out)
    got = swap(send, "core")
    (packed,) = call(pack_kernel, [((8 * NQ, H), BF16)], 3e8, 1.3e6)(keep, got)
    rows = exchange(packed.reshape(NQ, 8, H), CHIPS).reshape(8 * NQ, H)
    in_own, grad_own = call(split_kernel, [half] * 2, 3e8, 1.3e6)(rows)
    in_other = swap(in_own, "tp")
    grad_other = swap(grad_own, "tp")
    slope, out_keep, out_send = call(
        up_kernel, [((4 * NQ, FH), F32), half32, half], 1.7e9, 1e7
    )(ids, in_own, in_other, w_in, w_out)
    out_got = swap(out_send, "tp")
    pre_grad, in_keep, in_send = call(
        down_kernel, [((4 * NQ, FH), BF16), half32, half], 1.7e9, 1e7
    )(ids, grad_own, grad_other, slope, w_in, w_out)
    in_got = swap(in_send, "tp")
    grad_weight, weight_done = call(weight_kernel, [((1, D, FH), BF16), done], 8.4e8, 5e6)(
        ids, in_own, in_other, pre_grad
    )
    (merged,) = call(merge_kernel, [((8 * NQ, H), BF16)], 3e8, 2.6e6)(
        out_keep, out_got, in_keep, in_got, weight_done
    )
    rows = exchange(merged.reshape(NQ, 8, H), CHIPS).reshape(8 * NQ, H)
    own, send = call(unpack_kernel, [half] * 2, 3e8, 1.3e6)(rows)
    got = swap(send, "core")
    part, send = call(
        dots_kernel, [((B * M, E), F32), ((B * M, E), BF16)], 2 * small, 3e6
    )(own, got, tokens, grad_out, dispatch, combine)
    logit_got = swap(send, "tp")
    first, first_done = call(first_kernel, [((B, M, H), F32), done], small, 2e6)(
        own, got, dispatch
    )
    eight = ((8, H // 16, E), F32)
    logit, keep, send = call(
        logit_kernel,
        [((B * M, E), BF16), eight, eight],
        small,
        3e6,
        scratch=[pltpu.VMEM((H, E), F32)],
    )(ids, part, logit_got, tokens, first_done)
    got = swap(send, "core")
    grad_tokens, tokens_done = call(
        tokens_kernel, [((B, M, H), BF16), done], small, 3e6
    )(first, logit, ordered)
    (summed,) = call(add_kernel, [eight], 1e5, 5e5)(keep, got, tokens_done)
    summed = exchange(summed, ("x_hi", "y"))
    (summed,) = call(spread_kernel, [eight], 1e5, 5e5)(summed)
    summed = exchange(summed, "z")
    (summed,) = call(spread_kernel, [((16, H // 16, E), F32)], 1e5, 5e5)(summed)
    grad_router = exchange(summed, ("x_hi", "y", "core")).reshape(H, E)
    return grad_tokens, grad_router, grad_weight


def solution(mesh):
    fine = Mesh(mesh.devices.reshape(8, 2, 4, 2, 2), AXES)
    ep = ("z", "x_hi", "y", "core")
    return jax.shard_map(
        on_device,
        mesh=fine,
        in_specs=(
            P(ep, None, "tp"),
            P("tp", None),
            P(ep, None, "tp"),
            P(ep, "tp", None),
            P(ep, None, "tp"),
        ),
        out_specs=(P(ep, None, "tp"), P("tp", None), P(ep, None, "tp")),
        check_vma=False,
    )
```

```python
import jax
import jax.numpy as jnp
from jax import lax
from jax.experimental import pallas as pl
from jax.experimental.pallas import tpu as pltpu
from jax.sharding import Mesh, PartitionSpec as P

AXES = ("z2", "z1", "z0", "x_hi", "y", "core", "tp")
CHIPS = ("z2", "z1", "z0", "x_hi", "y")
F32 = jnp.float32
BF16 = jnp.bfloat16
I32 = jnp.int32
NQ = 64
B = 2
M = 256
E = 128
H = 640
D = 1280
FH = 1280
CH = 256
MIB = 1 << 20

SMEM = pl.BlockSpec(memory_space=pltpu.SMEM)
VMEM = pl.BlockSpec(memory_space=pltpu.VMEM)
HBM = pl.BlockSpec(memory_space=pltpu.HBM)


def dot(a, b):
    return jnp.dot(a, b, preferred_element_type=F32)


def dot_t(a, b):
    return lax.dot_general(a, b, (((1,), (1,)), ((), ())), preferred_element_type=F32)


def t_dot(a, b):
    return lax.dot_general(a, b, (((0,), (0,)), ((), ())), preferred_element_type=F32)


def rows_cols(rows, cols):
    return (
        lax.broadcasted_iota(I32, (rows, cols), 0),
        lax.broadcasted_iota(I32, (rows, cols), 1),
    )


def ones_where(mask):
    return jnp.where(mask, 1.0, 0.0).astype(BF16)


def expert_order(core):
    e, p = rows_cols(E, E)
    return ones_where(e == 2 * (p & 63) + (core ^ (p >> 6)))


def call(kernel, outs, flops, nbytes, hbm=(), scratch=(), limit=24):
    def run(*args):
        args = [
            pltpu.with_memory_space_constraint(a, pltpu.HBM) if i in hbm else a
            for i, a in enumerate(args)
        ]
        return pl.pallas_call(
            kernel,
            out_shape=[jax.ShapeDtypeStruct(s, d) for s, d in outs],
            in_specs=[
                SMEM if a.dtype == I32 else HBM if i in hbm else VMEM for i, a in enumerate(args)
            ],
            out_specs=[VMEM for _ in outs],
            scratch_shapes=list(scratch),
            cost_estimate=pl.CostEstimate(
                flops=int(flops), bytes_accessed=int(nbytes), transcendentals=0
            ),
            compiler_params=pltpu.CompilerParams(vmem_limit_bytes=limit * MIB),
        )(*args)

    return run


def logits_kernel(ids, tokens_hbm, router_hbm, part, ordered, tokens, router, sems):
    load = pltpu.make_async_copy(router_hbm, router, sems.at[4])
    load.start()
    copies = []
    for i in range(4):
        at = (i // 2, pl.ds((i % 2) * (M // 2), M // 2))
        copies.append(pltpu.make_async_copy(tokens_hbm.at[at], tokens.at[at], sems.at[i]))
        copies[i].start()
    order = expert_order(ids[0])
    load.wait()
    r = dot(router[...], order).astype(BF16)
    ordered[...] = r
    for b in range(B):
        copies[2 * b].wait()
        copies[2 * b + 1].wait()
        part[b * M : (b + 1) * M, :] = dot(tokens[b], r)


def fetch_kernel(grad_hbm, in_hbm, out_hbm, tokens, grad, w_in, w_out, turned, *rest):
    packing, splitting, merging, unpacking, sems = rest
    pairs = ((grad_hbm, grad), (in_hbm, w_in), (out_hbm, w_out))
    copies = [pltpu.make_async_copy(x, y, sems.at[i]) for i, (x, y) in enumerate(pairs)]
    for c in copies:
        c.start()
    for b in range(B):
        turned[:, b * M : (b + 1) * M] = jnp.transpose(tokens[b])
    i, j = rows_cols(8 * NQ, 8 * NQ)

    def packed_of_plain(j):
        return (j & 63) * 8 + (j >> 6)

    def packed_of_split(j):
        return (j & 63) * 8 + ((j >> 7) & 1) * 4 + (j >> 8) * 2 + ((j >> 6) & 1)

    packing[...] = ones_where(i == packed_of_plain(j))
    unpacking[...] = ones_where(j == packed_of_plain(i))
    merging[...] = ones_where(i == packed_of_split(j))
    splitting[...] = ones_where(j == packed_of_split(i))
    for c in copies:
        c.wait()


def slots_kernel(part, other, tokens, grad, dispatch, combine, keep, send):
    for b in range(B):
        rows = slice(b * M, (b + 1) * M)
        logits = part[rows, :] + other[rows, :]
        up = jnp.exp(logits - jnp.max(logits, axis=0, keepdims=True))
        d = up / jnp.sum(up, axis=0, keepdims=True)
        up = jnp.exp(logits - jnp.max(logits, axis=1, keepdims=True))
        c = up / jnp.sum(up, axis=1, keepdims=True)
        dispatch[rows, :] = d
        combine[rows, :] = c
        for a, (w, x) in enumerate(((d, tokens), (c, grad))):
            s = t_dot(w.astype(BF16), x[b]).astype(BF16)
            k = 2 * a + b
            keep[k * NQ : (k + 1) * NQ, :] = s[:NQ]
            send[k * NQ : (k + 1) * NQ, :] = s[NQ:]


def pack_kernel(packing, keep, got, out):
    n = 4 * NQ
    out[...] = (dot(packing[:, :n], keep[...]) + dot(packing[:, n:], got[...])).astype(BF16)


def split_kernel(splitting, rows, slot_in, slot_grad):
    n = 4 * NQ
    slot_in[...] = dot(splitting[:n, :], rows[...]).astype(BF16)
    slot_grad[...] = dot(splitting[n:, :], rows[...]).astype(BF16)


def both_halves(ids):
    t = ids[1]
    return (
        pl.ds(pl.multiple_of(t * H, 128), H),
        pl.ds(pl.multiple_of((1 - t) * H, 128), H),
    )


def up_kernel(ids, own, other, w_in, w_out, slope, out_keep, out_send):
    mine, theirs = both_halves(ids)
    x, y = own[...], other[...]
    keep = jnp.zeros((4 * NQ, H), F32)
    sent = jnp.zeros((4 * NQ, H), F32)
    for f in range(0, FH, CH):
        cols = slice(f, f + CH)
        v = dot(x, w_in[0, mine, cols]) + dot(y, w_in[0, theirs, cols])
        sq = v * v
        t = jnp.tanh(0.7978845608 * (v + 0.044715 * v * sq))
        act = (0.5 * v * (1.0 + t)).astype(BF16)
        slope[:, cols] = 0.5 * (1.0 + t) + 0.5 * v * (1.0 - t * t) * (
            0.7978845608 * (1.0 + 0.134145 * sq)
        )
        keep = keep + dot(act, w_out[0, cols, mine])
        sent = sent + dot(act, w_out[0, cols, theirs])
    out_keep[...] = keep
    out_send[...] = sent.astype(BF16)


def down_kernel(ids, own, other, slope, w_in, w_out, pre_grad, in_keep, in_send):
    mine, theirs = both_halves(ids)
    x, y = own[...], other[...]
    keep = jnp.zeros((4 * NQ, H), F32)
    sent = jnp.zeros((4 * NQ, H), F32)
    for f in range(0, FH, CH):
        cols = slice(f, f + CH)
        g = dot_t(x, w_out[0, cols, mine]) + dot_t(y, w_out[0, cols, theirs])
        g = (g * slope[:, cols]).astype(BF16)
        pre_grad[:, cols] = g
        keep = keep + dot_t(g, w_in[0, mine, cols])
        sent = sent + dot_t(g, w_in[0, theirs, cols])
    in_keep[...] = keep
    in_send[...] = sent.astype(BF16)


def weight_kernel(ids, own, other, pre_grad, out, done):
    for x, rows in zip((own, other), both_halves(ids)):
        out[0, rows, :] = t_dot(x[...], pre_grad[...]).astype(BF16)
    done[...] = jnp.zeros(done.shape, F32)


def merge_kernel(merging, out_keep, out_got, in_keep, in_got, done, out):
    n = 4 * NQ
    x = (out_keep[...] + out_got[...].astype(F32)).astype(BF16)
    y = (in_keep[...] + in_got[...].astype(F32)).astype(BF16)
    out[...] = (dot(merging[:, :n], x) + dot(merging[:, n:], y)).astype(BF16)


def unpack_kernel(unpacking, rows, own, send):
    n = 4 * NQ
    own[...] = dot(unpacking[:n, :], rows[...]).astype(BF16)
    send[...] = dot(unpacking[n:, :], rows[...]).astype(BF16)


def slots_of(own, got, a, b):
    rows = slice((2 * a + b) * NQ, (2 * a + b + 1) * NQ)
    return jnp.concatenate([own[rows, :], got[rows, :]], axis=0)


def dots_kernel(own, got, tokens, grad, dispatch, combine, part, send):
    for b in range(B):
        rows = slice(b * M, (b + 1) * M)
        c, d = combine[rows, :], dispatch[rows, :]
        x = dot_t(grad[b], slots_of(own, got, 0, b))
        y = dot_t(tokens[b], slots_of(own, got, 1, b))
        g = c * (x - jnp.sum(c * x, axis=1, keepdims=True))
        g = g + d * (y - jnp.sum(d * y, axis=0, keepdims=True))
        part[rows, :] = g
        send[rows, :] = g.astype(BF16)


def first_kernel(own, got, dispatch, out, done):
    for b in range(B):
        w = dispatch[b * M : (b + 1) * M, :].astype(BF16)
        out[b] = dot(w, slots_of(own, got, 1, b))
    done[...] = jnp.zeros(done.shape, F32)


def logit_kernel(ids, part, got, turned, done, logit, keep, send, whole):
    g = (part[...] + got[...].astype(F32)).astype(BF16)
    logit[...] = g
    plain = dot_t(g, expert_order(ids[0])).astype(BF16)
    whole[...] = dot(turned[...], plain)
    c = ids[0]
    n = H // 16
    for i in range(8):
        keep[i] = whole[pl.ds(pl.multiple_of((2 * i + c) * n, 8), n), :]
        send[i] = whole[pl.ds(pl.multiple_of((2 * i + 1 - c) * n, 8), n), :].astype(BF16)


def tokens_kernel(first, logit, router, out, done):
    for b in range(B):
        g = first[b] + dot_t(logit[b * M : (b + 1) * M, :], router[...])
        out[b] = g.astype(BF16)
    done[...] = jnp.zeros(done.shape, F32)


def add_kernel(x, y, done, out):
    out[...] = (x[...] + y[...].astype(F32)).astype(BF16)


def spread_kernel(x, out):
    total = x[0].astype(F32)
    for i in range(1, 8):
        total = total + x[i].astype(F32)
    total = total.astype(BF16)
    for i in range(out.shape[0]):
        out[i] = total


def widen_kernel(x, out):
    n = H // 16
    for i in range(16):
        out[i * n : (i + 1) * n, :] = x[i].astype(F32)


def swap(x, axis):
    return lax.ppermute(x, axis, [(0, 1), (1, 0)])


def exchange(x, axes):
    return lax.all_to_all(x, axes, split_axis=0, concat_axis=0, tiled=True)


def on_device(tokens, router, w_in, w_out, grad_out):
    ids = jnp.stack([lax.axis_index("core"), lax.axis_index("tp")]).astype(I32)
    half = ((4 * NQ, H), BF16)
    half32 = ((4 * NQ, H), F32)
    done = ((8, E), F32)
    small = 2 * B * M * H * E
    part, ordered, tokens = call(
        logits_kernel,
        [((B * M, E), F32), ((H, E), BF16), ((B, M, H), BF16)],
        small,
        1e6,
        hbm=(1, 2),
        scratch=[pltpu.VMEM((H, E), BF16), pltpu.SemaphoreType.DMA((5,))],
    )(ids, tokens, router)
    other = swap(part, "tp")
    onehot = ((8 * NQ, 8 * NQ), BF16)
    grad_out, w_in, w_out, turned, packing, splitting, merging, unpacking = call(
        fetch_kernel,
        [((B, M, H), BF16), ((1, D, FH), BF16), ((1, FH, D), BF16), ((H, B * M), BF16)]
        + [onehot] * 4,
        0,
        1.4e7,
        hbm=(0, 1, 2),
        scratch=[pltpu.SemaphoreType.DMA((3,))],
    )(grad_out, w_in, w_out, tokens)
    dispatch, combine, keep, send = call(
        slots_kernel, [((B * M, E), F32)] * 2 + [half] * 2, 2 * small, 3e6
    )(part, other, tokens, grad_out)
    got = swap(send, "core")
    (packed,) = call(pack_kernel, [((8 * NQ, H), BF16)], 3e8, 1.3e6)(packing, keep, got)
    rows = exchange(packed.reshape(NQ, 8, H), CHIPS).reshape(8 * NQ, H)
    in_own, grad_own = call(split_kernel, [half] * 2, 3e8, 1.3e6)(splitting, rows)
    in_other = swap(in_own, "tp")
    grad_other = swap(grad_own, "tp")
    slope, out_keep, out_send = call(
        up_kernel, [((4 * NQ, FH), F32), half32, half], 1.7e9, 1e7
    )(ids, in_own, in_other, w_in, w_out)
    out_got = swap(out_send, "tp")
    pre_grad, in_keep, in_send = call(
        down_kernel, [((4 * NQ, FH), BF16), half32, half], 1.7e9, 1e7
    )(ids, grad_own, grad_other, slope, w_in, w_out)
    in_got = swap(in_send, "tp")
    grad_weight, weight_done = call(weight_kernel, [((1, D, FH), BF16), done], 8.4e8, 5e6)(
        ids, in_own, in_other, pre_grad
    )
    (merged,) = call(merge_kernel, [((8 * NQ, H), BF16)], 3e8, 2.6e6)(
        merging, out_keep, out_got, in_keep, in_got, weight_done
    )
    rows = exchange(merged.reshape(NQ, 8, H), CHIPS).reshape(8 * NQ, H)
    own, send = call(unpack_kernel, [half] * 2, 3e8, 1.3e6)(unpacking, rows)
    got = swap(send, "core")
    part, send = call(
        dots_kernel, [((B * M, E), F32), ((B * M, E), BF16)], 2 * small, 3e6
    )(own, got, tokens, grad_out, dispatch, combine)
    logit_got = swap(send, "tp")
    first, first_done = call(first_kernel, [((B, M, H), F32), done], small, 2e6)(
        own, got, dispatch
    )
    eight = ((8, H // 16, E), BF16)
    eight32 = ((8, H // 16, E), F32)
    logit, keep, send = call(
        logit_kernel,
        [((B * M, E), BF16), eight32, eight],
        small,
        3e6,
        scratch=[pltpu.VMEM((H, E), F32)],
    )(ids, part, logit_got, turned, first_done)
    got = swap(send, "core")
    grad_tokens, tokens_done = call(
        tokens_kernel, [((B, M, H), BF16), done], small, 3e6
    )(first, logit, ordered)
    (summed,) = call(add_kernel, [eight], 1e5, 5e5)(keep, got, tokens_done)
    summed = exchange(summed, ("x_hi", "y"))
    (summed,) = call(spread_kernel, [eight], 1e5, 5e5)(summed)
    summed = exchange(summed, ("z0", "z1", "z2"))
    (summed,) = call(spread_kernel, [((16, H // 16, E), BF16)], 1e5, 5e5)(summed)
    summed = exchange(summed, ("x_hi", "y", "core"))
    (grad_router,) = call(widen_kernel, [((H, E), F32)], 1e5, 5e5)(summed)
    return grad_tokens, grad_router, grad_weight


def solution(mesh):
    fine = Mesh(mesh.devices.reshape(2, 2, 2, 2, 4, 2, 2), AXES)
    ep = CHIPS + ("core",)
    return jax.shard_map(
        on_device,
        mesh=fine,
        in_specs=(
            P(ep, None, "tp"),
            P("tp", None),
            P(ep, None, "tp"),
            P(ep, "tp", None),
            P(ep, None, "tp"),
        ),
        out_specs=(P(ep, None, "tp"), P("tp", None), P(ep, None, "tp")),
        check_vma=False,
    )
```

```python
import jax
import jax.numpy as jnp
from jax import lax
from jax.experimental import pallas as pl
from jax.experimental.pallas import tpu as pltpu
from jax.sharding import Mesh, PartitionSpec as P

AXES = ("z2", "z1", "z0", "x_hi", "y", "core", "tp")
CHIPS = ("z2", "z1", "z0", "x_hi", "y")
F32 = jnp.float32
BF16 = jnp.bfloat16
I32 = jnp.int32
NQ = 64
B = 2
M = 256
E = 128
H = 640
D = 1280
FH = 1280
CH = 256
MIB = 1 << 20

VMEM = pl.BlockSpec(memory_space=pltpu.VMEM)
HBM = pl.BlockSpec(memory_space=pltpu.HBM)


def dot(a, b):
    return jnp.dot(a, b, preferred_element_type=F32)


def dot_t(a, b):
    return lax.dot_general(a, b, (((1,), (1,)), ((), ())), preferred_element_type=F32)


def t_dot(a, b):
    return lax.dot_general(a, b, (((0,), (0,)), ((), ())), preferred_element_type=F32)


def rows_cols(rows, cols):
    return (
        lax.broadcasted_iota(I32, (rows, cols), 0),
        lax.broadcasted_iota(I32, (rows, cols), 1),
    )


def ones_where(mask):
    return jnp.where(mask, 1.0, 0.0).astype(BF16)


def expert_order(core):
    e, p = rows_cols(E, E)
    return ones_where(e == 2 * (p & 63) + (core ^ (p >> 6)))


def call(kernel, outs, flops, nbytes, hbm=(), scratch=(), limit=24):
    def run(*args):
        args = [
            pltpu.with_memory_space_constraint(a, pltpu.HBM) if i in hbm else a
            for i, a in enumerate(args)
        ]
        return pl.pallas_call(
            kernel,
            out_shape=[jax.ShapeDtypeStruct(s, d) for s, d in outs],
            in_specs=[
                HBM if i in hbm else VMEM for i in range(len(args))
            ],
            out_specs=[VMEM for _ in outs],
            scratch_shapes=list(scratch),
            cost_estimate=pl.CostEstimate(
                flops=int(flops), bytes_accessed=int(nbytes), transcendentals=0
            ),
            compiler_params=pltpu.CompilerParams(vmem_limit_bytes=limit * MIB),
        )(*args)

    return run


def logits_kernel(tokens_hbm, router_hbm, part, ordered, tokens, router, sems):
    load = pltpu.make_async_copy(router_hbm, router, sems.at[4])
    load.start()
    copies = []
    for i in range(4):
        at = (i // 2, pl.ds((i % 2) * (M // 2), M // 2))
        copies.append(pltpu.make_async_copy(tokens_hbm.at[at], tokens.at[at], sems.at[i]))
        copies[i].start()
    order = expert_order(lax.axis_index("core"))
    load.wait()
    r = dot(router[...], order).astype(BF16)
    ordered[...] = r
    for b in range(B):
        copies[2 * b].wait()
        copies[2 * b + 1].wait()
        part[b * M : (b + 1) * M, :] = dot(tokens[b], r)


def fetch_kernel(grad_hbm, in_hbm, out_hbm, tokens, grad, w_in, w_out, turned, sems):
    pairs = ((grad_hbm, grad), (in_hbm, w_in), (out_hbm, w_out))
    copies = [pltpu.make_async_copy(x, y, sems.at[i]) for i, (x, y) in enumerate(pairs)]
    for c in copies:
        c.start()
    for b in range(B):
        turned[:, b * M : (b + 1) * M] = jnp.transpose(tokens[b])
    for c in copies:
        c.wait()


def slots_kernel(part, other, tokens, grad, dispatch, combine, keep, send):
    for b in range(B):
        rows = slice(b * M, (b + 1) * M)
        logits = part[rows, :] + other[rows, :]
        up = jnp.exp(logits - jnp.max(logits, axis=0, keepdims=True))
        d = up / jnp.sum(up, axis=0, keepdims=True)
        up = jnp.exp(logits - jnp.max(logits, axis=1, keepdims=True))
        c = up / jnp.sum(up, axis=1, keepdims=True)
        dispatch[rows, :] = d
        combine[rows, :] = c
        for a, (w, x) in enumerate(((d, tokens), (c, grad))):
            s = t_dot(w.astype(BF16), x[b]).astype(BF16)
            k = 2 * a + b
            keep[k * NQ : (k + 1) * NQ, :] = s[:NQ]
            send[k * NQ : (k + 1) * NQ, :] = s[NQ:]


def interleave(pieces, out):
    i, j = rows_cols(E, E)
    to = ones_where(i == (j & 15) * 8 + (j >> 4))
    for g in range(0, NQ, 16):
        x = jnp.concatenate([x[n + g : n + g + 16, :] for x, n in pieces], axis=0)
        out[8 * g : 8 * g + E, :] = dot(to, x).astype(BF16)


def deinterleave(rows, pieces):
    i, j = rows_cols(E, E)
    to = ones_where(j == (i & 15) * 8 + (i >> 4))
    for g in range(0, NQ, 16):
        y = dot(to, rows[8 * g : 8 * g + E, :]).astype(BF16)
        for k, (x, n) in enumerate(pieces):
            x[n + g : n + g + 16, :] = y[16 * k : 16 * k + 16]


def pack_kernel(keep, got, out):
    interleave([(x, k * NQ) for x in (keep, got) for k in range(4)], out)


def by_image(x, y):
    return [(r, s * 2 * NQ + b * NQ) for s in range(2) for r in (x, y) for b in range(B)]


def split_kernel(rows, slot_in, slot_grad):
    deinterleave(rows, by_image(slot_in, slot_grad))


def both_halves():
    t = lax.axis_index("tp")
    return (
        pl.ds(pl.multiple_of(t * H, 128), H),
        pl.ds(pl.multiple_of((1 - t) * H, 128), H),
    )


def up_kernel(own, other, w_in, w_out, slope, out_keep, out_send):
    mine, theirs = both_halves()
    x, y = own[...], other[...]
    keep = jnp.zeros((4 * NQ, H), F32)
    sent = jnp.zeros((4 * NQ, H), F32)
    for f in range(0, FH, CH):
        cols = slice(f, f + CH)
        v = dot(x, w_in[0, mine, cols]) + dot(y, w_in[0, theirs, cols])
        sq = v * v
        t = jnp.tanh(0.7978845608 * (v + 0.044715 * v * sq))
        act = (0.5 * v * (1.0 + t)).astype(BF16)
        slope[:, cols] = 0.5 * (1.0 + t) + 0.5 * v * (1.0 - t * t) * (
            0.7978845608 * (1.0 + 0.134145 * sq)
        )
        keep = keep + dot(act, w_out[0, cols, mine])
        sent = sent + dot(act, w_out[0, cols, theirs])
    out_keep[...] = keep
    out_send[...] = sent.astype(BF16)


def down_kernel(own, other, slope, w_in, w_out, pre_grad, in_keep, in_send):
    mine, theirs = both_halves()
    x, y = own[...], other[...]
    keep = jnp.zeros((4 * NQ, H), F32)
    sent = jnp.zeros((4 * NQ, H), F32)
    for f in range(0, FH, CH):
        cols = slice(f, f + CH)
        g = dot_t(x, w_out[0, cols, mine]) + dot_t(y, w_out[0, cols, theirs])
        g = (g * slope[:, cols]).astype(BF16)
        pre_grad[:, cols] = g
        keep = keep + dot_t(g, w_in[0, mine, cols])
        sent = sent + dot_t(g, w_in[0, theirs, cols])
    in_keep[...] = keep
    in_send[...] = sent.astype(BF16)


def weight_kernel(own, other, pre_grad, out, done):
    for x, rows in zip((own, other), both_halves()):
        out[0, rows, :] = t_dot(x[...], pre_grad[...]).astype(BF16)
    done[...] = jnp.zeros(done.shape, F32)


def merge_kernel(out_keep, out_got, in_keep, in_got, done, out):
    x = (out_keep[...] + out_got[...].astype(F32)).astype(BF16)
    y = (in_keep[...] + in_got[...].astype(F32)).astype(BF16)
    interleave(by_image(x, y), out)


def unpack_kernel(rows, own, send):
    deinterleave(rows, [(x, k * NQ) for x in (own, send) for k in range(4)])


def slots_of(own, got, a, b):
    rows = slice((2 * a + b) * NQ, (2 * a + b + 1) * NQ)
    return jnp.concatenate([own[rows, :], got[rows, :]], axis=0)


def dots_kernel(own, got, tokens, grad, dispatch, combine, part, send):
    for b in range(B):
        rows = slice(b * M, (b + 1) * M)
        c, d = combine[rows, :], dispatch[rows, :]
        x = dot_t(grad[b], slots_of(own, got, 0, b))
        y = dot_t(tokens[b], slots_of(own, got, 1, b))
        g = c * (x - jnp.sum(c * x, axis=1, keepdims=True))
        g = g + d * (y - jnp.sum(d * y, axis=0, keepdims=True))
        part[rows, :] = g
        send[rows, :] = g.astype(BF16)


def first_kernel(own, got, dispatch, out, done):
    for b in range(B):
        w = dispatch[b * M : (b + 1) * M, :].astype(BF16)
        out[b] = dot(w, slots_of(own, got, 1, b))
    done[...] = jnp.zeros(done.shape, F32)


def logit_kernel(part, got, turned, done, logit, out):
    g = (part[...] + got[...].astype(F32)).astype(BF16)
    logit[...] = g
    plain = dot_t(g, expert_order(lax.axis_index("core"))).astype(BF16)
    total = dot(turned[...], plain)
    n = H // 16
    for i in range(16):
        out[i] = total[i * n : (i + 1) * n, :].astype(BF16)


def tokens_kernel(first, logit, router, out, done):
    for b in range(B):
        g = first[b] + dot_t(logit[b * M : (b + 1) * M, :], router[...])
        out[b] = g.astype(BF16)
    done[...] = jnp.zeros(done.shape, F32)


def sum_blocks(x):
    total = x[0].astype(F32)
    for i in range(1, x.shape[0]):
        total = total + x[i].astype(F32)
    return total.astype(BF16)


def early_kernel(x, done, out):
    total = sum_blocks(x)
    for i in range(out.shape[0]):
        out[i] = total


def late_kernel(x, out):
    total = sum_blocks(x)
    for i in range(out.shape[0]):
        out[i] = total


def widen_kernel(x, out):
    n = H // 16
    for i in range(16):
        out[i * n : (i + 1) * n, :] = x[i].astype(F32)


def swap(x, axis):
    return lax.ppermute(x, axis, [(0, 1), (1, 0)])


def exchange(x, axes):
    return lax.all_to_all(x, axes, split_axis=0, concat_axis=0, tiled=True)


def on_device(tokens, router, w_in, w_out, grad_out):
    half = ((4 * NQ, H), BF16)
    half32 = ((4 * NQ, H), F32)
    done = ((8, E), F32)
    small = 2 * B * M * H * E
    part, ordered, tokens = call(
        logits_kernel,
        [((B * M, E), F32), ((H, E), BF16), ((B, M, H), BF16)],
        small,
        1e6,
        hbm=(0, 1),
        scratch=[pltpu.VMEM((H, E), BF16), pltpu.SemaphoreType.DMA((5,))],
    )(tokens, router)
    other = swap(part, "tp")
    grad_out, w_in, w_out, turned = call(
        fetch_kernel,
        [((B, M, H), BF16), ((1, D, FH), BF16), ((1, FH, D), BF16), ((H, B * M), BF16)],
        0,
        1.4e7,
        hbm=(0, 1, 2),
        scratch=[pltpu.SemaphoreType.DMA((3,))],
    )(grad_out, w_in, w_out, tokens)
    dispatch, combine, keep, send = call(
        slots_kernel, [((B * M, E), F32)] * 2 + [half] * 2, 2 * small, 3e6
    )(part, other, tokens, grad_out)
    got = swap(send, "core")
    (packed,) = call(pack_kernel, [((8 * NQ, H), BF16)], 3e8, 1.3e6)(keep, got)
    rows = exchange(packed.reshape(NQ, 8, H), CHIPS).reshape(8 * NQ, H)
    in_own, grad_own = call(split_kernel, [half] * 2, 3e8, 1.3e6)(rows)
    in_other = swap(in_own, "tp")
    grad_other = swap(grad_own, "tp")
    slope, out_keep, out_send = call(
        up_kernel, [((4 * NQ, FH), F32), half32, half], 1.7e9, 1e7
    )(in_own, in_other, w_in, w_out)
    out_got = swap(out_send, "tp")
    pre_grad, in_keep, in_send = call(
        down_kernel, [((4 * NQ, FH), BF16), half32, half], 1.7e9, 1e7
    )(grad_own, grad_other, slope, w_in, w_out)
    in_got = swap(in_send, "tp")
    grad_weight, weight_done = call(weight_kernel, [((1, D, FH), BF16), done], 8.4e8, 5e6)(
        in_own, in_other, pre_grad
    )
    (merged,) = call(merge_kernel, [((8 * NQ, H), BF16)], 3e8, 2.6e6)(
        out_keep, out_got, in_keep, in_got, weight_done
    )
    rows = exchange(merged.reshape(NQ, 8, H), CHIPS).reshape(8 * NQ, H)
    own, send = call(unpack_kernel, [half] * 2, 3e8, 1.3e6)(rows)
    got = swap(send, "core")
    part, send = call(
        dots_kernel, [((B * M, E), F32), ((B * M, E), BF16)], 2 * small, 3e6
    )(own, got, tokens, grad_out, dispatch, combine)
    logit_got = swap(send, "tp")
    first, first_done = call(first_kernel, [((B, M, H), F32), done], small, 2e6)(
        own, got, dispatch
    )
    eight = ((8, H // 16, E), BF16)
    sixteen = ((16, H // 16, E), BF16)
    plane = ("x_hi", "y", "core")
    logit, blocks = call(logit_kernel, [((B * M, E), BF16), sixteen], small, 3e6)(
        part, logit_got, turned, first_done
    )
    blocks = exchange(blocks, plane)
    grad_tokens, tokens_done = call(
        tokens_kernel, [((B, M, H), BF16), done], small, 3e6
    )(first, logit, ordered)
    (blocks,) = call(early_kernel, [eight], 1e5, 5e5)(blocks, tokens_done)
    blocks = exchange(blocks, ("z0", "z1", "z2"))
    (blocks,) = call(late_kernel, [sixteen], 1e5, 5e5)(blocks)
    blocks = exchange(blocks, plane)
    (grad_router,) = call(widen_kernel, [((H, E), F32)], 1e5, 5e5)(blocks)
    return grad_tokens, grad_router, grad_weight


def solution(mesh):
    fine = Mesh(mesh.devices.reshape(2, 2, 2, 2, 4, 2, 2), AXES)
    ep = CHIPS + ("core",)
    return jax.shard_map(
        on_device,
        mesh=fine,
        in_specs=(
            P(ep, None, "tp"),
            P("tp", None),
            P(ep, None, "tp"),
            P(ep, "tp", None),
            P(ep, None, "tp"),
        ),
        out_specs=(P(ep, None, "tp"), P("tp", None), P(ep, None, "tp")),
        check_vma=False,
    )
```

```python
import jax
import jax.numpy as jnp
from jax import lax
from jax.experimental import pallas as pl
from jax.experimental.pallas import tpu as pltpu
from jax.sharding import Mesh, PartitionSpec as P

AXES = ("z2", "z1", "z0", "x_hi", "y", "core", "tp")
CHIPS = ("z2", "z1", "z0", "x_hi", "y")
F32 = jnp.float32
BF16 = jnp.bfloat16
I32 = jnp.int32
NQ = 64
B = 2
M = 256
E = 128
H = 640
D = 1280
FH = 1280
CH = 256
MIB = 1 << 20

VMEM = pl.BlockSpec(memory_space=pltpu.VMEM)
HBM = pl.BlockSpec(memory_space=pltpu.HBM)


def dot(a, b):
    return jnp.dot(a, b, preferred_element_type=F32)


def dot_t(a, b):
    return lax.dot_general(a, b, (((1,), (1,)), ((), ())), preferred_element_type=F32)


def t_dot(a, b):
    return lax.dot_general(a, b, (((0,), (0,)), ((), ())), preferred_element_type=F32)


def rows_cols(rows, cols):
    return (
        lax.broadcasted_iota(I32, (rows, cols), 0),
        lax.broadcasted_iota(I32, (rows, cols), 1),
    )


def ones_where(mask):
    return jnp.where(mask, 1.0, 0.0).astype(BF16)


def expert_order(core):
    e, p = rows_cols(E, E)
    return ones_where(e == 2 * (p & 63) + (core ^ (p >> 6)))


def call(kernel, outs, flops, nbytes, hbm=(), scratch=(), out_space=VMEM, limit=24):
    def run(*args):
        args = [
            pltpu.with_memory_space_constraint(a, pltpu.HBM) if i in hbm else a
            for i, a in enumerate(args)
        ]
        return pl.pallas_call(
            kernel,
            out_shape=[jax.ShapeDtypeStruct(s, d) for s, d in outs],
            in_specs=[
                HBM if i in hbm else VMEM for i in range(len(args))
            ],
            out_specs=[out_space for _ in outs],
            scratch_shapes=list(scratch),
            cost_estimate=pl.CostEstimate(
                flops=int(flops), bytes_accessed=int(nbytes), transcendentals=0
            ),
            compiler_params=pltpu.CompilerParams(vmem_limit_bytes=limit * MIB),
        )(*args)

    return run


def logits_kernel(tokens_hbm, router_hbm, part, ordered, tokens, router, sems):
    load = pltpu.make_async_copy(router_hbm, router, sems.at[4])
    load.start()
    copies = []
    for i in range(4):
        at = (i // 2, pl.ds((i % 2) * (M // 2), M // 2))
        copies.append(pltpu.make_async_copy(tokens_hbm.at[at], tokens.at[at], sems.at[i]))
        copies[i].start()
    order = expert_order(lax.axis_index("core"))
    load.wait()
    r = dot(router[...], order).astype(BF16)
    ordered[...] = jnp.transpose(r)
    for b in range(B):
        copies[2 * b].wait()
        copies[2 * b + 1].wait()
        part[b * M : (b + 1) * M, :] = dot(tokens[b], r)


def fetch_kernel(grad_hbm, in_hbm, out_hbm, tokens, grad, w_in, w_out, turned, sems):
    pairs = ((grad_hbm, grad), (in_hbm, w_in), (out_hbm, w_out))
    copies = [pltpu.make_async_copy(x, y, sems.at[i]) for i, (x, y) in enumerate(pairs)]
    for c in copies:
        c.start()
    for b in range(B):
        turned[:, b * M : (b + 1) * M] = jnp.transpose(tokens[b])
    for c in copies:
        c.wait()


def slots_kernel(part, other, tokens, grad, dispatch, combine, keep, send):
    for b in range(B):
        rows = slice(b * M, (b + 1) * M)
        logits = part[rows, :] + other[rows, :]
        up = jnp.exp(logits - jnp.max(logits, axis=0, keepdims=True))
        d = up / jnp.sum(up, axis=0, keepdims=True)
        up = jnp.exp(logits - jnp.max(logits, axis=1, keepdims=True))
        c = up / jnp.sum(up, axis=1, keepdims=True)
        dispatch[rows, :] = d
        combine[rows, :] = c
        for a, (w, x) in enumerate(((d, tokens), (c, grad))):
            s = t_dot(w.astype(BF16), x[b]).astype(BF16)
            k = 2 * a + b
            keep[k * NQ : (k + 1) * NQ, :] = s[:NQ]
            send[k * NQ : (k + 1) * NQ, :] = s[NQ:]


def interleave(pieces, out):
    i, j = rows_cols(E, E)
    to = ones_where(i == (j & 15) * 8 + (j >> 4))
    for g in range(0, NQ, 16):
        x = jnp.concatenate([x[n + g : n + g + 16, :] for x, n in pieces], axis=0)
        out[8 * g : 8 * g + E, :] = dot(to, x).astype(BF16)


def deinterleave(rows, pieces):
    i, j = rows_cols(E, E)
    to = ones_where(j == (i & 15) * 8 + (i >> 4))
    for g in range(0, NQ, 16):
        y = dot(to, rows[8 * g : 8 * g + E, :]).astype(BF16)
        for k, (x, n) in enumerate(pieces):
            x[n + g : n + g + 16, :] = y[16 * k : 16 * k + 16]


def pack_kernel(keep, got, out):
    interleave([(x, k * NQ) for x in (keep, got) for k in range(4)], out)


def by_image(x, y):
    return [(r, s * 2 * NQ + b * NQ) for s in range(2) for r in (x, y) for b in range(B)]


def split_kernel(rows, slot_in, slot_grad):
    deinterleave(rows, by_image(slot_in, slot_grad))


def both_halves():
    t = lax.axis_index("tp")
    return (
        pl.ds(pl.multiple_of(t * H, 128), H),
        pl.ds(pl.multiple_of((1 - t) * H, 128), H),
    )


def up_kernel(own, other, w_in, w_out, slope, out_keep, out_send, total):
    mine, theirs = both_halves()
    x, y = own[...], other[...]
    for f in range(0, FH, CH):
        cols = slice(f, f + CH)
        v = dot(x, w_in[0, mine, cols]) + dot(y, w_in[0, theirs, cols])
        sq = v * v
        t = jnp.tanh(0.7978845608 * (v + 0.044715 * v * sq))
        act = (0.5 * v * (1.0 + t)).astype(BF16)
        slope[:, cols] = 0.5 * (1.0 + t) + 0.5 * v * (1.0 - t * t) * (
            0.7978845608 * (1.0 + 0.134145 * sq)
        )
        p = dot(act, w_out[0, cols, :])
        total[...] = p if f == 0 else total[...] + p
    out_keep[...] = total[:, mine]
    out_send[...] = total[:, theirs].astype(BF16)


def down_kernel(own, other, slope, w_in, w_out, pre_grad, in_keep, in_send, total):
    mine, theirs = both_halves()
    x, y = own[...], other[...]
    for f in range(0, FH, CH):
        cols = slice(f, f + CH)
        g = dot_t(x, w_out[0, cols, mine]) + dot_t(y, w_out[0, cols, theirs])
        g = (g * slope[:, cols]).astype(BF16)
        pre_grad[:, cols] = g
        p = dot_t(g, w_in[0, :, cols])
        total[...] = p if f == 0 else total[...] + p
    in_keep[...] = total[:, mine]
    in_send[...] = total[:, theirs].astype(BF16)


def weight_kernel(own, other, pre_grad, out, done):
    for x, rows in zip((own, other), both_halves()):
        out[0, rows, :] = t_dot(x[...], pre_grad[...]).astype(BF16)
    done[...] = jnp.zeros(done.shape, F32)


def merge_kernel(out_keep, out_got, in_keep, in_got, done, out):
    x = (out_keep[...] + out_got[...].astype(F32)).astype(BF16)
    y = (in_keep[...] + in_got[...].astype(F32)).astype(BF16)
    interleave(by_image(x, y), out)


def unpack_kernel(rows, own, send):
    deinterleave(rows, [(x, k * NQ) for x in (own, send) for k in range(4)])


def slots_of(own, got, a, b):
    rows = slice((2 * a + b) * NQ, (2 * a + b + 1) * NQ)
    return jnp.concatenate([own[rows, :], got[rows, :]], axis=0)


def dots_kernel(own, got, tokens, grad, dispatch, combine, part, send):
    for b in range(B):
        rows = slice(b * M, (b + 1) * M)
        c, d = combine[rows, :], dispatch[rows, :]
        x = dot_t(grad[b], slots_of(own, got, 0, b))
        y = dot_t(tokens[b], slots_of(own, got, 1, b))
        g = c * (x - jnp.sum(c * x, axis=1, keepdims=True))
        g = g + d * (y - jnp.sum(d * y, axis=0, keepdims=True))
        part[rows, :] = g
        send[rows, :] = g.astype(BF16)


def first_kernel(own, got, dispatch, out, done):
    for b in range(B):
        w = dispatch[b * M : (b + 1) * M, :].astype(BF16)
        out[b] = dot(w, slots_of(own, got, 1, b))
    done[...] = jnp.zeros(done.shape, F32)


def logit_kernel(part, got, turned, done, logit, out):
    g = (part[...] + got[...].astype(F32)).astype(BF16)
    logit[...] = g
    plain = dot_t(g, expert_order(lax.axis_index("core"))).astype(BF16)
    total = dot(turned[...], plain)
    n = H // 16
    for i in range(16):
        out[i] = total[i * n : (i + 1) * n, :].astype(BF16)


def sum_blocks(x):
    total = x[0].astype(F32)
    for i in range(1, x.shape[0]):
        total = total + x[i].astype(F32)
    return total.astype(BF16)


def spread_kernel(x, out):
    total = sum_blocks(x)
    for i in range(out.shape[0]):
        out[i] = total


def last_kernel(x, first, logit, ordered, router_hbm, tokens_hbm, router, tokens, sems):
    copies = []
    for b in range(B):
        g = first[b] + dot(logit[b * M : (b + 1) * M, :], ordered[...])
        tokens[b] = g.astype(BF16)
        copies.append(pltpu.make_async_copy(tokens.at[b], tokens_hbm.at[b], sems.at[b]))
        copies[b].start()
    n = H // 16
    for i in range(16):
        router[i * n : (i + 1) * n, :] = x[i].astype(F32)
    copies.append(pltpu.make_async_copy(router, router_hbm, sems.at[2]))
    copies[2].start()
    for c in copies:
        c.wait()


def swap(x, axis):
    return lax.ppermute(x, axis, [(0, 1), (1, 0)])


def exchange(x, axes):
    return lax.all_to_all(x, axes, split_axis=0, concat_axis=0, tiled=True)


def on_device(tokens, router, w_in, w_out, grad_out):
    half = ((4 * NQ, H), BF16)
    half32 = ((4 * NQ, H), F32)
    total = [pltpu.VMEM((4 * NQ, D), F32)]
    done = ((8, E), F32)
    small = 2 * B * M * H * E
    part, ordered, tokens = call(
        logits_kernel,
        [((B * M, E), F32), ((E, H), BF16), ((B, M, H), BF16)],
        small,
        1e6,
        hbm=(0, 1),
        scratch=[pltpu.VMEM((H, E), BF16), pltpu.SemaphoreType.DMA((5,))],
    )(tokens, router)
    other = swap(part, "tp")
    grad_out, w_in, w_out, turned = call(
        fetch_kernel,
        [((B, M, H), BF16), ((1, D, FH), BF16), ((1, FH, D), BF16), ((H, B * M), BF16)],
        0,
        1.4e7,
        hbm=(0, 1, 2),
        scratch=[pltpu.SemaphoreType.DMA((3,))],
    )(grad_out, w_in, w_out, tokens)
    dispatch, combine, keep, send = call(
        slots_kernel, [((B * M, E), F32)] * 2 + [half] * 2, 2 * small, 3e6
    )(part, other, tokens, grad_out)
    got = swap(send, "core")
    (packed,) = call(pack_kernel, [((8 * NQ, H), BF16)], 3e8, 1.3e6)(keep, got)
    rows = exchange(packed.reshape(NQ, 8, H), CHIPS).reshape(8 * NQ, H)
    in_own, grad_own = call(split_kernel, [half] * 2, 3e8, 1.3e6)(rows)
    in_other = swap(in_own, "tp")
    grad_other = swap(grad_own, "tp")
    slope, out_keep, out_send = call(
        up_kernel, [((4 * NQ, FH), F32), half32, half], 1.7e9, 1e7, scratch=total
    )(in_own, in_other, w_in, w_out)
    out_got = swap(out_send, "tp")
    pre_grad, in_keep, in_send = call(
        down_kernel, [((4 * NQ, FH), BF16), half32, half], 1.7e9, 1e7, scratch=total
    )(grad_own, grad_other, slope, w_in, w_out)
    in_got = swap(in_send, "tp")
    grad_weight, weight_done = call(weight_kernel, [((1, D, FH), BF16), done], 8.4e8, 5e6)(
        in_own, in_other, pre_grad
    )
    (merged,) = call(merge_kernel, [((8 * NQ, H), BF16)], 3e8, 2.6e6)(
        out_keep, out_got, in_keep, in_got, weight_done
    )
    rows = exchange(merged.reshape(NQ, 8, H), CHIPS).reshape(8 * NQ, H)
    own, send = call(unpack_kernel, [half] * 2, 3e8, 1.3e6)(rows)
    got = swap(send, "core")
    part, send = call(
        dots_kernel, [((B * M, E), F32), ((B * M, E), BF16)], 2 * small, 3e6
    )(own, got, tokens, grad_out, dispatch, combine)
    logit_got = swap(send, "tp")
    first, first_done = call(first_kernel, [((B, M, H), F32), done], small, 2e6)(
        own, got, dispatch
    )
    eight = ((8, H // 16, E), BF16)
    sixteen = ((16, H // 16, E), BF16)
    plane = ("x_hi", "y", "core")
    logit, blocks = call(logit_kernel, [((B * M, E), BF16), sixteen], small, 3e6)(
        part, logit_got, turned, first_done
    )
    blocks = exchange(blocks, plane)
    (blocks,) = call(spread_kernel, [eight], 1e5, 5e5)(blocks)
    blocks = exchange(blocks, ("z0", "z1", "z2"))
    (blocks,) = call(spread_kernel, [sixteen], 1e5, 5e5)(blocks)
    blocks = exchange(blocks, plane)
    grad_router, grad_tokens = call(
        last_kernel,
        [((H, E), F32), ((B, M, H), BF16)],
        small,
        3e6,
        scratch=[
            pltpu.VMEM((H, E), F32),
            pltpu.VMEM((B, M, H), BF16),
            pltpu.SemaphoreType.DMA((3,)),
        ],
        out_space=HBM,
    )(blocks, first, logit, ordered)
    return grad_tokens, grad_router, grad_weight


def solution(mesh):
    fine = Mesh(mesh.devices.reshape(2, 2, 2, 2, 4, 2, 2), AXES)
    ep = CHIPS + ("core",)
    return jax.shard_map(
        on_device,
        mesh=fine,
        in_specs=(
            P(ep, None, "tp"),
            P("tp", None),
            P(ep, None, "tp"),
            P(ep, "tp", None),
            P(ep, None, "tp"),
        ),
        out_specs=(P(ep, None, "tp"), P("tp", None), P(ep, None, "tp")),
        check_vma=False,
    )
```

```python
import jax
import jax.numpy as jnp
from jax import lax
from jax.experimental import pallas as pl
from jax.experimental.pallas import tpu as pltpu
from jax.sharding import Mesh, PartitionSpec as P

AXES = ("z2", "z1", "z0", "x_hi", "y", "core", "tp")
CHIPS = ("z2", "z1", "z0", "x_hi", "y")
F32 = jnp.float32
BF16 = jnp.bfloat16
I32 = jnp.int32
NQ = 64
B = 2
M = 256
E = 128
H = 640
D = 1280
FH = 1280
CH = 256
MIB = 1 << 20

VMEM = pl.BlockSpec(memory_space=pltpu.VMEM)
HBM = pl.BlockSpec(memory_space=pltpu.HBM)


def dot(a, b):
    return jnp.dot(a, b, preferred_element_type=F32)


def dot_t(a, b):
    return lax.dot_general(a, b, (((1,), (1,)), ((), ())), preferred_element_type=F32)


def t_dot(a, b):
    return lax.dot_general(a, b, (((0,), (0,)), ((), ())), preferred_element_type=F32)


def rows_cols(rows, cols):
    return (
        lax.broadcasted_iota(I32, (rows, cols), 0),
        lax.broadcasted_iota(I32, (rows, cols), 1),
    )


def ones_where(mask):
    return jnp.where(mask, 1.0, 0.0).astype(BF16)


def expert_order(core):
    e, p = rows_cols(E, E)
    return ones_where(e == 2 * (p & 63) + (core ^ (p >> 6)))


def call(kernel, outs, flops, nbytes, hbm=(), scratch=(), limit=24):
    def run(*args):
        args = [
            pltpu.with_memory_space_constraint(a, pltpu.HBM) if i in hbm else a
            for i, a in enumerate(args)
        ]
        return pl.pallas_call(
            kernel,
            out_shape=[jax.ShapeDtypeStruct(s, d) for s, d in outs],
            in_specs=[
                HBM if i in hbm else VMEM for i in range(len(args))
            ],
            out_specs=[VMEM for _ in outs],
            scratch_shapes=list(scratch),
            cost_estimate=pl.CostEstimate(
                flops=int(flops), bytes_accessed=int(nbytes), transcendentals=0
            ),
            compiler_params=pltpu.CompilerParams(vmem_limit_bytes=limit * MIB),
        )(*args)

    return run


def logits_kernel(tokens_hbm, router_hbm, part, ordered, tokens, router, sems):
    load = pltpu.make_async_copy(router_hbm, router, sems.at[4])
    load.start()
    copies = []
    for i in range(4):
        at = (i // 2, pl.ds((i % 2) * (M // 2), M // 2))
        copies.append(pltpu.make_async_copy(tokens_hbm.at[at], tokens.at[at], sems.at[i]))
        copies[i].start()
    order = expert_order(lax.axis_index("core"))
    load.wait()
    r = dot(router[...], order).astype(BF16)
    ordered[...] = r
    for b in range(B):
        copies[2 * b].wait()
        copies[2 * b + 1].wait()
        part[b * M : (b + 1) * M, :] = dot(tokens[b], r)


def fetch_kernel(grad_hbm, in_hbm, out_hbm, tokens, grad, w_in, w_out, turned, sems):
    pairs = ((grad_hbm, grad), (in_hbm, w_in), (out_hbm, w_out))
    copies = [pltpu.make_async_copy(x, y, sems.at[i]) for i, (x, y) in enumerate(pairs)]
    for c in copies:
        c.start()
    for b in range(B):
        turned[:, b * M : (b + 1) * M] = jnp.transpose(tokens[b])
    for c in copies:
        c.wait()


def slots_kernel(part, other, tokens, grad, dispatch, combine, keep, send):
    for b in range(B):
        rows = slice(b * M, (b + 1) * M)
        logits = part[rows, :] + other[rows, :]
        up = jnp.exp(logits - jnp.max(logits, axis=0, keepdims=True))
        d = up / jnp.sum(up, axis=0, keepdims=True)
        up = jnp.exp(logits - jnp.max(logits, axis=1, keepdims=True))
        c = up / jnp.sum(up, axis=1, keepdims=True)
        dispatch[rows, :] = d
        combine[rows, :] = c
        for a, (w, x) in enumerate(((d, tokens), (c, grad))):
            s = t_dot(w.astype(BF16), x[b]).astype(BF16)
            k = 2 * a + b
            keep[k * NQ : (k + 1) * NQ, :] = s[:NQ]
            send[k * NQ : (k + 1) * NQ, :] = s[NQ:]


def interleave(pieces, out):
    i, j = rows_cols(E, E)
    to = ones_where(i == (j & 15) * 8 + (j >> 4))
    for g in range(0, NQ, 16):
        x = jnp.concatenate([x[n + g : n + g + 16, :] for x, n in pieces], axis=0)
        out[8 * g : 8 * g + E, :] = dot(to, x).astype(BF16)


def deinterleave(rows, pieces):
    i, j = rows_cols(E, E)
    to = ones_where(j == (i & 15) * 8 + (i >> 4))
    for g in range(0, NQ, 16):
        y = dot(to, rows[8 * g : 8 * g + E, :]).astype(BF16)
        for k, (x, n) in enumerate(pieces):
            x[n + g : n + g + 16, :] = y[16 * k : 16 * k + 16]


def pack_kernel(keep, got, out):
    interleave([(x, k * NQ) for x in (keep, got) for k in range(4)], out)


def by_image(x, y):
    return [(r, s * 2 * NQ + b * NQ) for s in range(2) for r in (x, y) for b in range(B)]


def split_kernel(rows, slot_in, slot_grad):
    deinterleave(rows, by_image(slot_in, slot_grad))


def both_halves():
    t = lax.axis_index("tp")
    return (
        pl.ds(pl.multiple_of(t * H, 128), H),
        pl.ds(pl.multiple_of((1 - t) * H, 128), H),
    )


def up_kernel(own, other, w_in, w_out, slope, out_keep, out_send, total):
    mine, theirs = both_halves()
    x, y = own[...], other[...]
    for f in range(0, FH, CH):
        cols = slice(f, f + CH)
        v = dot(x, w_in[0, mine, cols]) + dot(y, w_in[0, theirs, cols])
        sq = v * v
        t = jnp.tanh(0.7978845608 * (v + 0.044715 * v * sq))
        act = (0.5 * v * (1.0 + t)).astype(BF16)
        slope[:, cols] = 0.5 * (1.0 + t) + 0.5 * v * (1.0 - t * t) * (
            0.7978845608 * (1.0 + 0.134145 * sq)
        )
        p = dot(act, w_out[0, cols, :])
        total[...] = p if f == 0 else total[...] + p
    out_keep[...] = total[:, mine]
    out_send[...] = total[:, theirs].astype(BF16)


def down_kernel(own, other, slope, w_in, w_out, pre_grad, in_keep, in_send, total):
    mine, theirs = both_halves()
    x, y = own[...], other[...]
    for f in range(0, FH, CH):
        cols = slice(f, f + CH)
        g = dot_t(x, w_out[0, cols, mine]) + dot_t(y, w_out[0, cols, theirs])
        g = (g * slope[:, cols]).astype(BF16)
        pre_grad[:, cols] = g
        p = dot_t(g, w_in[0, :, cols])
        total[...] = p if f == 0 else total[...] + p
    in_keep[...] = total[:, mine]
    in_send[...] = total[:, theirs].astype(BF16)


def weight_kernel(own, other, pre_grad, out, done):
    for x, rows in zip((own, other), both_halves()):
        out[0, rows, :] = t_dot(x[...], pre_grad[...]).astype(BF16)
    done[...] = jnp.zeros(done.shape, F32)


def merge_kernel(out_keep, out_got, in_keep, in_got, done, out):
    x = (out_keep[...] + out_got[...].astype(F32)).astype(BF16)
    y = (in_keep[...] + in_got[...].astype(F32)).astype(BF16)
    interleave(by_image(x, y), out)


def unpack_kernel(rows, own, send):
    deinterleave(rows, [(x, k * NQ) for x in (own, send) for k in range(4)])


def slots_of(own, got, a, b):
    rows = slice((2 * a + b) * NQ, (2 * a + b + 1) * NQ)
    return jnp.concatenate([own[rows, :], got[rows, :]], axis=0)


def dots_kernel(own, got, tokens, grad, dispatch, combine, part, send):
    for b in range(B):
        rows = slice(b * M, (b + 1) * M)
        c, d = combine[rows, :], dispatch[rows, :]
        x = dot_t(grad[b], slots_of(own, got, 0, b))
        y = dot_t(tokens[b], slots_of(own, got, 1, b))
        g = c * (x - jnp.sum(c * x, axis=1, keepdims=True))
        g = g + d * (y - jnp.sum(d * y, axis=0, keepdims=True))
        part[rows, :] = g
        send[rows, :] = g.astype(BF16)


def first_kernel(own, got, dispatch, out, done):
    for b in range(B):
        w = dispatch[b * M : (b + 1) * M, :].astype(BF16)
        out[b] = dot(w, slots_of(own, got, 1, b))
    done[...] = jnp.zeros(done.shape, F32)


def logit_kernel(part, got, turned, done, logit, out):
    g = (part[...] + got[...].astype(F32)).astype(BF16)
    logit[...] = g
    plain = dot_t(g, expert_order(lax.axis_index("core"))).astype(BF16)
    total = dot(turned[...], plain)
    n = H // 16
    for i in range(16):
        out[i] = total[i * n : (i + 1) * n, :].astype(BF16)


def tokens_kernel(first, logit, router, out, done):
    for b in range(B):
        g = first[b] + dot_t(logit[b * M : (b + 1) * M, :], router[...])
        out[b] = g.astype(BF16)
    done[...] = jnp.zeros(done.shape, F32)


def sum_blocks(x):
    total = x[0].astype(F32)
    for i in range(1, x.shape[0]):
        total = total + x[i].astype(F32)
    return total.astype(BF16)


def early_kernel(x, done, out):
    total = sum_blocks(x)
    for i in range(out.shape[0]):
        out[i] = total


def late_kernel(x, out):
    total = sum_blocks(x)
    for i in range(out.shape[0]):
        out[i] = total


def widen_kernel(x, out):
    n = H // 16
    for i in range(16):
        out[i * n : (i + 1) * n, :] = x[i].astype(F32)


def swap(x, axis):
    return lax.ppermute(x, axis, [(0, 1), (1, 0)])


def exchange(x, axes):
    return lax.all_to_all(x, axes, split_axis=0, concat_axis=0, tiled=True)


def on_device(tokens, router, w_in, w_out, grad_out):
    half = ((4 * NQ, H), BF16)
    half32 = ((4 * NQ, H), F32)
    total = [pltpu.VMEM((4 * NQ, D), F32)]
    done = ((8, E), F32)
    small = 2 * B * M * H * E
    part, ordered, tokens = call(
        logits_kernel,
        [((B * M, E), F32), ((H, E), BF16), ((B, M, H), BF16)],
        small,
        1e6,
        hbm=(0, 1),
        scratch=[pltpu.VMEM((H, E), BF16), pltpu.SemaphoreType.DMA((5,))],
    )(tokens, router)
    other = swap(part, "tp")
    grad_out, w_in, w_out, turned = call(
        fetch_kernel,
        [((B, M, H), BF16), ((1, D, FH), BF16), ((1, FH, D), BF16), ((H, B * M), BF16)],
        0,
        1.4e7,
        hbm=(0, 1, 2),
        scratch=[pltpu.SemaphoreType.DMA((3,))],
    )(grad_out, w_in, w_out, tokens)
    dispatch, combine, keep, send = call(
        slots_kernel, [((B * M, E), F32)] * 2 + [half] * 2, 2 * small, 3e6
    )(part, other, tokens, grad_out)
    got = swap(send, "core")
    (packed,) = call(pack_kernel, [((8 * NQ, H), BF16)], 3e8, 1.3e6)(keep, got)
    rows = exchange(packed.reshape(NQ, 8, H), CHIPS).reshape(8 * NQ, H)
    in_own, grad_own = call(split_kernel, [half] * 2, 3e8, 1.3e6)(rows)
    in_other = swap(in_own, "tp")
    grad_other = swap(grad_own, "tp")
    slope, out_keep, out_send = call(
        up_kernel, [((4 * NQ, FH), F32), half32, half], 1.7e9, 1e7, scratch=total
    )(in_own, in_other, w_in, w_out)
    out_got = swap(out_send, "tp")
    pre_grad, in_keep, in_send = call(
        down_kernel, [((4 * NQ, FH), BF16), half32, half], 1.7e9, 1e7, scratch=total
    )(grad_own, grad_other, slope, w_in, w_out)
    in_got = swap(in_send, "tp")
    grad_weight, weight_done = call(weight_kernel, [((1, D, FH), BF16), done], 8.4e8, 5e6)(
        in_own, in_other, pre_grad
    )
    (merged,) = call(merge_kernel, [((8 * NQ, H), BF16)], 3e8, 2.6e6)(
        out_keep, out_got, in_keep, in_got, weight_done
    )
    rows = exchange(merged.reshape(NQ, 8, H), CHIPS).reshape(8 * NQ, H)
    own, send = call(unpack_kernel, [half] * 2, 3e8, 1.3e6)(rows)
    got = swap(send, "core")
    part, send = call(
        dots_kernel, [((B * M, E), F32), ((B * M, E), BF16)], 2 * small, 3e6
    )(own, got, tokens, grad_out, dispatch, combine)
    logit_got = swap(send, "tp")
    first, first_done = call(first_kernel, [((B, M, H), F32), done], small, 2e6)(
        own, got, dispatch
    )
    eight = ((8, H // 16, E), BF16)
    sixteen = ((16, H // 16, E), BF16)
    plane = ("x_hi", "y", "core")
    logit, blocks = call(logit_kernel, [((B * M, E), BF16), sixteen], small, 3e6)(
        part, logit_got, turned, first_done
    )
    blocks = exchange(blocks, plane)
    grad_tokens, tokens_done = call(
        tokens_kernel, [((B, M, H), BF16), done], small, 3e6
    )(first, logit, ordered)
    (blocks,) = call(early_kernel, [eight], 1e5, 5e5)(blocks, tokens_done)
    blocks = exchange(blocks, ("z0", "z1", "z2"))
    (blocks,) = call(late_kernel, [sixteen], 1e5, 5e5)(blocks)
    blocks = exchange(blocks, plane)
    (grad_router,) = call(widen_kernel, [((H, E), F32)], 1e5, 5e5)(blocks)
    return grad_tokens, grad_router, grad_weight


def solution(mesh):
    fine = Mesh(mesh.devices.reshape(2, 2, 2, 2, 4, 2, 2), AXES)
    ep = CHIPS + ("core",)
    return jax.shard_map(
        on_device,
        mesh=fine,
        in_specs=(
            P(ep, None, "tp"),
            P("tp", None),
            P(ep, None, "tp"),
            P(ep, "tp", None),
            P(ep, None, "tp"),
        ),
        out_specs=(P(ep, None, "tp"), P("tp", None), P(ep, None, "tp")),
        check_vma=False,
    )
```

```python
import jax
import jax.numpy as jnp
from jax import lax
from jax.experimental import pallas as pl
from jax.experimental.pallas import tpu as pltpu
from jax.sharding import Mesh, PartitionSpec as P

AXES = ("z2", "z1", "z0", "x_hi", "y", "core", "tp")
CHIPS = ("z2", "z1", "z0", "x_hi", "y")
F32 = jnp.float32
BF16 = jnp.bfloat16
I32 = jnp.int32
NQ = 64
B = 2
M = 256
E = 128
H = 640
D = 1280
FH = 1280
CH = 256
MIB = 1 << 20

VMEM = pl.BlockSpec(memory_space=pltpu.VMEM)
HBM = pl.BlockSpec(memory_space=pltpu.HBM)


def dot(a, b):
    return jnp.dot(a, b, preferred_element_type=F32)


def dot_t(a, b):
    return lax.dot_general(a, b, (((1,), (1,)), ((), ())), preferred_element_type=F32)


def t_dot(a, b):
    return lax.dot_general(a, b, (((0,), (0,)), ((), ())), preferred_element_type=F32)


def rows_cols(rows, cols):
    return (
        lax.broadcasted_iota(I32, (rows, cols), 0),
        lax.broadcasted_iota(I32, (rows, cols), 1),
    )


def ones_where(mask):
    return jnp.where(mask, 1.0, 0.0).astype(BF16)


def expert_order(core):
    e, p = rows_cols(E, E)
    return ones_where(e == 2 * (p & 63) + (core ^ (p >> 6)))


def call(kernel, outs, flops, nbytes, hbm=(), scratch=(), out_space=VMEM, limit=24):
    def run(*args):
        args = [
            pltpu.with_memory_space_constraint(a, pltpu.HBM) if i in hbm else a
            for i, a in enumerate(args)
        ]
        return pl.pallas_call(
            kernel,
            out_shape=[jax.ShapeDtypeStruct(s, d) for s, d in outs],
            in_specs=[
                HBM if i in hbm else VMEM for i in range(len(args))
            ],
            out_specs=[out_space for _ in outs],
            scratch_shapes=list(scratch),
            cost_estimate=pl.CostEstimate(
                flops=int(flops), bytes_accessed=int(nbytes), transcendentals=0
            ),
            compiler_params=pltpu.CompilerParams(vmem_limit_bytes=limit * MIB),
        )(*args)

    return run


def logits_kernel(tokens_hbm, router_hbm, part, ordered, tokens, router, sems):
    load = pltpu.make_async_copy(router_hbm, router, sems.at[4])
    load.start()
    copies = []
    for i in range(4):
        at = (i // 2, pl.ds((i % 2) * (M // 2), M // 2))
        copies.append(pltpu.make_async_copy(tokens_hbm.at[at], tokens.at[at], sems.at[i]))
        copies[i].start()
    order = expert_order(lax.axis_index("core"))
    load.wait()
    r = dot(router[...], order).astype(BF16)
    ordered[...] = jnp.transpose(r)
    for b in range(B):
        copies[2 * b].wait()
        copies[2 * b + 1].wait()
        part[b * M : (b + 1) * M, :] = dot(tokens[b], r)


def fetch_kernel(grad_hbm, in_hbm, out_hbm, tokens, grad, w_in, w_out, turned, sems):
    pairs = ((grad_hbm, grad), (in_hbm, w_in), (out_hbm, w_out))
    copies = [pltpu.make_async_copy(x, y, sems.at[i]) for i, (x, y) in enumerate(pairs)]
    for c in copies:
        c.start()
    for b in range(B):
        turned[:, b * M : (b + 1) * M] = jnp.transpose(tokens[b])
    for c in copies:
        c.wait()


def slots_kernel(part, other, tokens, grad, dispatch, combine, keep, send):
    for b in range(B):
        rows = slice(b * M, (b + 1) * M)
        logits = part[rows, :] + other[rows, :]
        up = jnp.exp(logits - jnp.max(logits, axis=0, keepdims=True))
        d = up / jnp.sum(up, axis=0, keepdims=True)
        up = jnp.exp(logits - jnp.max(logits, axis=1, keepdims=True))
        c = up / jnp.sum(up, axis=1, keepdims=True)
        dispatch[rows, :] = d
        combine[rows, :] = c
        for a, (w, x) in enumerate(((d, tokens), (c, grad))):
            s = t_dot(w.astype(BF16), x[b]).astype(BF16)
            k = 2 * a + b
            keep[k * NQ : (k + 1) * NQ, :] = s[:NQ]
            send[k * NQ : (k + 1) * NQ, :] = s[NQ:]


def interleave(pieces, out):
    i, j = rows_cols(E, E)
    to = ones_where(i == (j & 15) * 8 + (j >> 4))
    for g in range(0, NQ, 16):
        x = jnp.concatenate([x[n + g : n + g + 16, :] for x, n in pieces], axis=0)
        out[8 * g : 8 * g + E, :] = dot(to, x).astype(BF16)


def deinterleave(rows, pieces):
    i, j = rows_cols(E, E)
    to = ones_where(j == (i & 15) * 8 + (i >> 4))
    for g in range(0, NQ, 16):
        y = dot(to, rows[8 * g : 8 * g + E, :]).astype(BF16)
        for k, (x, n) in enumerate(pieces):
            x[n + g : n + g + 16, :] = y[16 * k : 16 * k + 16]


def pack_kernel(keep, got, out):
    interleave([(x, k * NQ) for x in (keep, got) for k in range(4)], out)


def by_image(x, y):
    return [(r, s * 2 * NQ + b * NQ) for s in range(2) for r in (x, y) for b in range(B)]


def split_kernel(rows, slot_in, slot_grad):
    deinterleave(rows, by_image(slot_in, slot_grad))


def both_halves():
    t = lax.axis_index("tp")
    return (
        pl.ds(pl.multiple_of(t * H, 128), H),
        pl.ds(pl.multiple_of((1 - t) * H, 128), H),
    )


def up_kernel(own, other, w_in, w_out, slope, out_keep, out_send):
    mine, theirs = both_halves()
    x, y = own[...], other[...]
    keep = jnp.zeros((4 * NQ, H), F32)
    sent = jnp.zeros((4 * NQ, H), F32)
    for f in range(0, FH, CH):
        cols = slice(f, f + CH)
        v = dot(x, w_in[0, mine, cols]) + dot(y, w_in[0, theirs, cols])
        sq = v * v
        t = jnp.tanh(0.7978845608 * (v + 0.044715 * v * sq))
        act = (0.5 * v * (1.0 + t)).astype(BF16)
        slope[:, cols] = 0.5 * (1.0 + t) + 0.5 * v * (1.0 - t * t) * (
            0.7978845608 * (1.0 + 0.134145 * sq)
        )
        keep = keep + dot(act, w_out[0, cols, mine])
        sent = sent + dot(act, w_out[0, cols, theirs])
    out_keep[...] = keep
    out_send[...] = sent.astype(BF16)


def down_kernel(own, other, slope, w_in, w_out, pre_grad, in_keep, in_send):
    mine, theirs = both_halves()
    x, y = own[...], other[...]
    keep = jnp.zeros((4 * NQ, H), F32)
    sent = jnp.zeros((4 * NQ, H), F32)
    for f in range(0, FH, CH):
        cols = slice(f, f + CH)
        g = dot_t(x, w_out[0, cols, mine]) + dot_t(y, w_out[0, cols, theirs])
        g = (g * slope[:, cols]).astype(BF16)
        pre_grad[:, cols] = g
        keep = keep + dot_t(g, w_in[0, mine, cols])
        sent = sent + dot_t(g, w_in[0, theirs, cols])
    in_keep[...] = keep
    in_send[...] = sent.astype(BF16)


def weight_kernel(own, other, pre_grad, out, done):
    for x, rows in zip((own, other), both_halves()):
        out[0, rows, :] = t_dot(x[...], pre_grad[...]).astype(BF16)
    done[...] = jnp.zeros(done.shape, F32)


def merge_kernel(out_keep, out_got, in_keep, in_got, done, out):
    x = (out_keep[...] + out_got[...].astype(F32)).astype(BF16)
    y = (in_keep[...] + in_got[...].astype(F32)).astype(BF16)
    interleave(by_image(x, y), out)


def unpack_kernel(rows, own, send):
    deinterleave(rows, [(x, k * NQ) for x in (own, send) for k in range(4)])


def slots_of(own, got, a, b):
    rows = slice((2 * a + b) * NQ, (2 * a + b + 1) * NQ)
    return jnp.concatenate([own[rows, :], got[rows, :]], axis=0)


def dots_kernel(own, got, tokens, grad, dispatch, combine, part, send):
    for b in range(B):
        rows = slice(b * M, (b + 1) * M)
        c, d = combine[rows, :], dispatch[rows, :]
        x = dot_t(grad[b], slots_of(own, got, 0, b))
        y = dot_t(tokens[b], slots_of(own, got, 1, b))
        g = c * (x - jnp.sum(c * x, axis=1, keepdims=True))
        g = g + d * (y - jnp.sum(d * y, axis=0, keepdims=True))
        part[rows, :] = g
        send[rows, :] = g.astype(BF16)


def first_kernel(own, got, dispatch, out, done):
    for b in range(B):
        w = dispatch[b * M : (b + 1) * M, :].astype(BF16)
        out[b] = dot(w, slots_of(own, got, 1, b))
    done[...] = jnp.zeros(done.shape, F32)


def logit_kernel(part, got, turned, done, logit, out):
    g = (part[...] + got[...].astype(F32)).astype(BF16)
    logit[...] = g
    plain = dot_t(g, expert_order(lax.axis_index("core"))).astype(BF16)
    total = dot(turned[...], plain)
    n = H // 16
    for i in range(16):
        out[i] = total[i * n : (i + 1) * n, :].astype(BF16)


def sum_blocks(x):
    total = x[0].astype(F32)
    for i in range(1, x.shape[0]):
        total = total + x[i].astype(F32)
    return total.astype(BF16)


def spread_kernel(x, out):
    total = sum_blocks(x)
    for i in range(out.shape[0]):
        out[i] = total


def last_kernel(x, first, logit, ordered, router_hbm, tokens_hbm, router, tokens, sems):
    copies = []
    for b in range(B):
        g = first[b] + dot(logit[b * M : (b + 1) * M, :], ordered[...])
        tokens[b] = g.astype(BF16)
        copies.append(pltpu.make_async_copy(tokens.at[b], tokens_hbm.at[b], sems.at[b]))
        copies[b].start()
    n = H // 16
    for i in range(16):
        router[i * n : (i + 1) * n, :] = x[i].astype(F32)
    copies.append(pltpu.make_async_copy(router, router_hbm, sems.at[2]))
    copies[2].start()
    for c in copies:
        c.wait()


def swap(x, axis):
    return lax.ppermute(x, axis, [(0, 1), (1, 0)])


def exchange(x, axes):
    return lax.all_to_all(x, axes, split_axis=0, concat_axis=0, tiled=True)


def on_device(tokens, router, w_in, w_out, grad_out):
    half = ((4 * NQ, H), BF16)
    half32 = ((4 * NQ, H), F32)
    done = ((8, E), F32)
    small = 2 * B * M * H * E
    part, ordered, tokens = call(
        logits_kernel,
        [((B * M, E), F32), ((E, H), BF16), ((B, M, H), BF16)],
        small,
        1e6,
        hbm=(0, 1),
        scratch=[pltpu.VMEM((H, E), BF16), pltpu.SemaphoreType.DMA((5,))],
    )(tokens, router)
    other = swap(part, "tp")
    grad_out, w_in, w_out, turned = call(
        fetch_kernel,
        [((B, M, H), BF16), ((1, D, FH), BF16), ((1, FH, D), BF16), ((H, B * M), BF16)],
        0,
        1.4e7,
        hbm=(0, 1, 2),
        scratch=[pltpu.SemaphoreType.DMA((3,))],
    )(grad_out, w_in, w_out, tokens)
    dispatch, combine, keep, send = call(
        slots_kernel, [((B * M, E), F32)] * 2 + [half] * 2, 2 * small, 3e6
    )(part, other, tokens, grad_out)
    got = swap(send, "core")
    (packed,) = call(pack_kernel, [((8 * NQ, H), BF16)], 3e8, 1.3e6)(keep, got)
    rows = exchange(packed.reshape(NQ, 8, H), CHIPS).reshape(8 * NQ, H)
    in_own, grad_own = call(split_kernel, [half] * 2, 3e8, 1.3e6)(rows)
    in_other = swap(in_own, "tp")
    grad_other = swap(grad_own, "tp")
    slope, out_keep, out_send = call(
        up_kernel, [((4 * NQ, FH), F32), half32, half], 1.7e9, 1e7
    )(in_own, in_other, w_in, w_out)
    out_got = swap(out_send, "tp")
    pre_grad, in_keep, in_send = call(
        down_kernel, [((4 * NQ, FH), BF16), half32, half], 1.7e9, 1e7
    )(grad_own, grad_other, slope, w_in, w_out)
    in_got = swap(in_send, "tp")
    grad_weight, weight_done = call(weight_kernel, [((1, D, FH), BF16), done], 8.4e8, 5e6)(
        in_own, in_other, pre_grad
    )
    (merged,) = call(merge_kernel, [((8 * NQ, H), BF16)], 3e8, 2.6e6)(
        out_keep, out_got, in_keep, in_got, weight_done
    )
    rows = exchange(merged.reshape(NQ, 8, H), CHIPS).reshape(8 * NQ, H)
    own, send = call(unpack_kernel, [half] * 2, 3e8, 1.3e6)(rows)
    got = swap(send, "core")
    part, send = call(
        dots_kernel, [((B * M, E), F32), ((B * M, E), BF16)], 2 * small, 3e6
    )(own, got, tokens, grad_out, dispatch, combine)
    logit_got = swap(send, "tp")
    first, first_done = call(first_kernel, [((B, M, H), F32), done], small, 2e6)(
        own, got, dispatch
    )
    eight = ((8, H // 16, E), BF16)
    sixteen = ((16, H // 16, E), BF16)
    plane = ("x_hi", "y", "core")
    logit, blocks = call(logit_kernel, [((B * M, E), BF16), sixteen], small, 3e6)(
        part, logit_got, turned, first_done
    )
    blocks = exchange(blocks, plane)
    (blocks,) = call(spread_kernel, [eight], 1e5, 5e5)(blocks)
    blocks = exchange(blocks, ("z0", "z1", "z2"))
    (blocks,) = call(spread_kernel, [sixteen], 1e5, 5e5)(blocks)
    blocks = exchange(blocks, plane)
    grad_router, grad_tokens = call(
        last_kernel,
        [((H, E), F32), ((B, M, H), BF16)],
        small,
        3e6,
        scratch=[
            pltpu.VMEM((H, E), F32),
            pltpu.VMEM((B, M, H), BF16),
            pltpu.SemaphoreType.DMA((3,)),
        ],
        out_space=HBM,
    )(blocks, first, logit, ordered)
    return grad_tokens, grad_router, grad_weight


def solution(mesh):
    fine = Mesh(mesh.devices.reshape(2, 2, 2, 2, 4, 2, 2), AXES)
    ep = CHIPS + ("core",)
    return jax.shard_map(
        on_device,
        mesh=fine,
        in_specs=(
            P(ep, None, "tp"),
            P("tp", None),
            P(ep, None, "tp"),
            P(ep, "tp", None),
            P(ep, None, "tp"),
        ),
        out_specs=(P(ep, None, "tp"), P("tp", None), P(ep, None, "tp")),
        check_vma=False,
    )
```
